32 devices in a mesh: head: 2 (over x), blk: 16 (over z, y, core).
Axes of the slice: x: 2, y: 2, z: 4, core: 2. Of those that a mesh axis runs over, the one named last changes fastest.
Arguments:
- hidden_in: bfloat16 [512, 2048], P('blk'), may hold values from -6 to 6
- attn_gain: float32 [2048], replicated, may hold values from 0.25 to 1.75
- w_query: bfloat16 [1536, 2048], P('head'), may hold values from -0.125 to 0.125
- w_latent: bfloat16 [576, 2048], P('head'), may hold values from -0.125 to 0.125
- kv_gain: float32 [512], replicated, may hold values from 0.25 to 1.75
- w_key_up: bfloat16 [512, 1024], P(None, 'head'), may hold values from -0.25 to 0.25
- w_value_up: bfloat16 [512, 1024], P(None, 'head'), may hold values from -0.25 to 0.25
- w_out: bfloat16 [1024, 2048], P('head'), may hold values from -0.1875 to 0.1875
- cache_rows: bfloat16 [6144, 576], P('blk'), may hold values from -6 to 6
- slot_request: int32 [48], P('blk'), may hold values from -1 to 15, as said below
- slot_block: int32 [48], P('blk'), may hold values from 0 to 16
- lengths: int32 [16], replicated, may hold values from 1 to 2176, as said below
- parents: int32 [16, 32], P('blk'), may hold values from -1 to 30, as said below
- accepted: int32 [16, 8], P('blk'), may hold values from 0 to 28, as said below
- new_slots: int32 [16, 8], P('blk'), may hold values from 0 to 255, as said below
- moe_gain: float32 [2048], replicated, may hold values from 0.25 to 1.75
- routes: int32 [512, 6], P('blk'), may hold values from 0 to 15, all different within a row; in each aligned block of 32 rows (0 to 31, 32 to 63, ...) at most 24 rows name the same one
- route_logits: float32 [512, 6], P('blk'), may hold values from -8 to 8
- w_gate: bfloat16 [16, 1408, 2048], P('blk', 'head'), may hold values from -0.125 to 0.125
- w_up: bfloat16 [16, 1408, 2048], P('blk', 'head'), may hold values from -0.125 to 0.125
- w_down: bfloat16 [16, 1408, 2048], P('blk', 'head'), may hold values from -0.15625 to 0.15625
Outputs:
- layer_out: bfloat16 [512, 2048], P('blk')
- new_rows: bfloat16 [256, 576], P('blk')
The draws below stay inside these ranges and needn't reach their ends.
Inputs may be any that keep to these rules, and one draw needn't show every extreme that they name: A pool slot holds block slot_block of request slot_request or is free (-1); each request's blocks are distinct slots. Request r holds exactly ceil(lengths[r] / 128) pool blocks, numbered 0 upwards; one request holds 17 full blocks. `parents`: entry 0 of each request is -1 (the root); entry i names one of the tokens i - 4 .. i - 1. `accepted`: the first 8 tokens of a path from the root down the request's tree, root first. `new_slots`: all distinct. `routes`: within the 32 rows of one index of blk no expert is named more than 24 times.
All inputs are finite; a program needn't handle non-finite values.
Results may differ from the reference program's by a relative error of at most 0.0075.
Values may be sent and summed in bfloat16 or wider, within the bound.
No kernel may reach another device: no remote copies, remote signals or barrier semaphores. Data moves between devices by JAX's collectives and lax.ppermute only.
A program may use at most 128 MiB of HBM per device.

```python
import math
import jax
import jax.numpy as jnp
import numpy as np
from jax import lax

D = 2048
HEADS = 8
NOPE = 128
ROPE = 64
VDIM = 128
RANK = 512
FF = 1408
TOPK = 6
BLOCK = 128
DRAFT = 32
ACC = 8
TOK_DEV = 32
REQS = 16
TOKENS = 512
POOL = 48
MAXB = 17
EXPERTS = 16
CAP = 24
NEW_ROWS = 256
N_BLK = 16


def layout_parts(key):
    key_base = jax.random.fold_in(key, 11)
    key_long = jax.random.fold_in(key, 12)
    key_perm = jax.random.fold_in(key, 13)
    key_tail = jax.random.fold_in(key, 14)
    request_ids = jnp.arange(REQS, dtype=jnp.int32)
    longest = jax.random.randint(key_long, (), 0, REQS, dtype=jnp.int32)
    counts = 1 + jax.random.randint(key_base, (REQS,), 0, 2, dtype=jnp.int32)
    counts = jnp.where(request_ids == longest, MAXB, counts)
    offsets = jnp.cumsum(counts) - counts
    block_ids = jnp.arange(MAXB, dtype=jnp.int32)
    order = jax.random.permutation(key_perm, POOL).astype(jnp.int32)
    flat_pos = offsets[:, None] + block_ids[None, :]
    valid = block_ids[None, :] < counts[:, None]
    target = jnp.where(valid, order[jnp.minimum(flat_pos, POOL - 1)], POOL).reshape(-1)
    owners = jnp.broadcast_to(request_ids[:, None], (REQS, MAXB)).reshape(-1)
    positions = jnp.broadcast_to(block_ids[None, :], (REQS, MAXB)).reshape(-1)
    slot_request = jnp.full((POOL,), -1, jnp.int32).at[target].set(owners, mode='drop')
    slot_block = jnp.zeros((POOL,), jnp.int32).at[target].set(positions, mode='drop')
    tail = jax.random.randint(key_tail, (REQS,), 1, BLOCK + 1, dtype=jnp.int32)
    lengths = jnp.where(request_ids == longest, MAXB * BLOCK, (counts - 1) * BLOCK + tail)
    return (slot_request, slot_block, lengths)


def tree_parts(key):
    key_parent = jax.random.fold_in(key, 21)
    key_leaf = jax.random.fold_in(key, 22)
    key_chain = jax.random.fold_in(key, 23)
    nodes = jnp.arange(DRAFT, dtype=jnp.int32)
    request_ids = jnp.arange(REQS, dtype=jnp.int32)
    chained = jax.random.randint(key_chain, (), 0, REQS, dtype=jnp.int32)
    lower = jnp.maximum(nodes - 4, 0)
    upper = jnp.maximum(nodes, 1)
    picks = jax.random.randint(key_parent, (REQS, DRAFT), lower, upper, dtype=jnp.int32)
    picks = jnp.where((request_ids == chained)[:, None], lower[None, :], picks)
    parents = jnp.where(nodes[None, :] == 0, -1, picks)
    current = jax.random.randint(key_leaf, (REQS,), DRAFT - 4, DRAFT, dtype=jnp.int32)
    current = jnp.where(request_ids == chained, DRAFT - 4, current)
    walked = []
    for section in range(DRAFT):
        walked.append(current)
        above = jnp.take_along_axis(parents, current[:, None], axis=1)[:, 0]
        current = jnp.maximum(above, 0)
    walk = jnp.stack(walked, axis=1)
    depth = jnp.sum((walk > 0).astype(jnp.int32), axis=1)
    steps_back = depth[:, None] - jnp.arange(ACC, dtype=jnp.int32)[None, :]
    accepted = jnp.take_along_axis(walk, steps_back, axis=1)
    return (parents, accepted)


def draw_slot_request(key, part):
    return layout_parts(key)[0]


def draw_slot_block(key, part):
    return layout_parts(key)[1]


def draw_lengths(key, part):
    return layout_parts(key)[2]


def draw_parents(key, part):
    return tree_parts(key)[0]


def draw_accepted(key, part):
    return tree_parts(key)[1]


def draw_new_slots(key, part):
    order = jax.random.permutation(jax.random.fold_in(key, 31), NEW_ROWS).astype(jnp.int32)
    return order[:REQS * ACC].reshape(REQS, ACC)


def block_levels(rng, dims, cuts, least, top_value):
    factor_of = 1.0
    for axis_at, blocks in cuts:
        heights = jax.random.uniform(jax.random.fold_in(jax.random.fold_in(rng, 6), axis_at), (blocks,), jnp.float32, least / len(cuts), top_value / len(cuts))
        factor_of = factor_of * jnp.repeat(jnp.exp(heights), dims[axis_at] // blocks).reshape((-1,) + (1,) * (len(dims) - 1 - axis_at))
    return factor_of


def shared_out(rng, own, number, rows, count, top, limit, skew):
    ranking = jax.random.permutation(rng, count)
    packed, ordinary = shares(count, rows * top, limit, skew, True), shares(count, rows * top, limit, skew, False)
    places = jnp.arange(count)

    def named(sizes, rotation):
        used = int((sizes > 0).sum())
        fixed = max(1, used // 4)
        moved = fixed + (places - fixed + rotation * (used - fixed)) % max(1, count - fixed)
        return jnp.zeros((count,), jnp.int32).at[ranking[jnp.where(places < fixed, places, moved)]].set(jnp.asarray(sizes, jnp.int32))

    sizes = jnp.where(number % 4 == 0, named(packed, number // 4), named(ordinary, number - number // 4 - 1))
    mixed = jax.random.permutation(jax.random.fold_in(own, 3), count)
    source_of, receiver = mixed[0:count // 2 * 2:2], mixed[1:count // 2 * 2:2]
    room = jnp.minimum(sizes[source_of] - 1, limit - sizes[receiver]) // 2
    room = jnp.where((source_of == ranking[0]) | (receiver == ranking[0]) | (sizes[receiver] == 0), 0, jnp.maximum(room, 0))
    moved = jax.random.randint(jax.random.fold_in(own, 4), (count // 2,), 0, 1 << 20) % (room + 1)
    sizes = sizes.at[source_of].add(-moved).at[receiver].add(moved)
    items = jnp.searchsorted(jnp.cumsum(sizes), jnp.arange(rows * top), side="right").astype(jnp.int32)
    listing = items.reshape(top, rows).T
    listing = listing[jax.random.permutation(jax.random.fold_in(own, 1), rows)]
    rotation = jax.random.randint(jax.random.fold_in(own, 2), (rows, 1), 0, top)
    return jnp.take_along_axis(listing, (jnp.arange(top)[None, :] + rotation) % top, axis=1)


def shares(amount, total, bound, skew, full):
    weights = [(1 << 20) // math.isqrt(grade ** skew) + 1 for grade in range(1, amount + 1)]
    largest = bound if full else min(bound, max(-(-total // amount), total * weights[0] // sum(weights)))
    least = 1 if total - largest >= amount - 1 else 0
    holding, rest = [largest] + [least] * (amount - 1), total - largest - least * (amount - 1)
    while rest > 0:
        movable = [i for i in range(1, amount) if holding[i] < largest] or [i for i in range(1, amount) if holding[i] < bound]
        mass, budget = sum([weights[i] for i in movable]), rest
        for i in movable:
            addition = min(bound - holding[i], max(1, budget * weights[i] // mass), rest)
            holding[i] = holding[i] + addition
            rest = rest - addition
    return np.array(holding)


def noise(key, dims, spread, bound, pieces=(), kind=jnp.bfloat16):
    values = spread * jax.random.normal(key, dims, jnp.float32)
    if pieces:
        values = values * block_levels(key, dims, pieces, -0.22, 0.18)
    return jnp.clip(values, -bound, bound).astype(kind)


def setup_inputs(seed: int = 0) -> dict:
    keys = jax.random.split(jax.random.key(seed), 22)
    hidden_in = noise(keys[0], (TOKENS, D), 1.0, 6.0, ((0, 16),))
    attn_gain = jnp.clip(1.0 + 0.15 * jax.random.normal(keys[1], (D,), jnp.float32), 0.25, 1.75)
    w_query = noise(keys[2], (HEADS * (NOPE + ROPE), D), D ** -0.5, 0.125, ((0, 2),))
    w_latent = noise(keys[3], (RANK + ROPE, D), D ** -0.5, 0.125, ((0, 2),))
    kv_gain = jnp.clip(1.0 + 0.15 * jax.random.normal(keys[4], (RANK,), jnp.float32), 0.25, 1.75)
    w_key_up = noise(keys[5], (RANK, HEADS * NOPE), RANK ** -0.5, 0.25, ((1, 2),))
    w_value_up = noise(keys[6], (RANK, HEADS * VDIM), RANK ** -0.5, 0.25, ((1, 2),))
    w_out = noise(keys[7], (HEADS * VDIM, D), (HEADS * VDIM) ** -0.5, 0.1875, ((0, 2),))
    cache_rows = noise(keys[8], (POOL * BLOCK, RANK + ROPE), 1.0, 6.0, ((0, 16),))
    slot_request = draw_slot_request(jax.random.fold_in(keys[21], 71), 0)
    slot_block = draw_slot_block(jax.random.fold_in(keys[21], 71), 0)
    lengths = draw_lengths(jax.random.fold_in(keys[21], 71), 0)
    parents = draw_parents(jax.random.fold_in(keys[21], 71), 0)
    accepted = draw_accepted(jax.random.fold_in(keys[21], 71), 0)
    new_slots = draw_new_slots(jax.random.fold_in(keys[21], 71), 0)
    moe_gain = jnp.clip(1.0 + 0.15 * jax.random.normal(keys[15], (D,), jnp.float32), 0.25, 1.75)
    routes_keys = jax.random.split(jax.random.fold_in(keys[16], 1), TOKENS // TOK_DEV)
    routes_turns = jax.random.permutation(jax.random.fold_in(keys[16], 3), TOKENS // TOK_DEV)
    routes = jax.vmap(lambda own, number: shared_out(jax.random.fold_in(keys[16], 2), own, number, TOK_DEV, EXPERTS, TOPK, CAP, 2))(routes_keys, routes_turns).reshape((TOKENS, TOPK))
    route_logits = noise(keys[17], (TOKENS, TOPK), 2.0, 8.0, ((0, 16),), jnp.float32)
    w_gate = noise(keys[18], (EXPERTS, FF, D), D ** -0.5, 0.125, ((0, 16), (1, 2)))
    w_up = noise(keys[19], (EXPERTS, FF, D), D ** -0.5, 0.125, ((0, 16), (1, 2)))
    w_down = noise(keys[20], (EXPERTS, FF, D), FF ** -0.5, 0.15625, ((0, 16), (1, 2)))
    return {"hidden_in": hidden_in, "attn_gain": attn_gain, "w_query": w_query, "w_latent": w_latent, "kv_gain": kv_gain, "w_key_up": w_key_up, "w_value_up": w_value_up, "w_out": w_out, "cache_rows": cache_rows, "slot_request": slot_request, "slot_block": slot_block, "lengths": lengths, "parents": parents, "accepted": accepted, "new_slots": new_slots, "moe_gain": moe_gain, "routes": routes, "route_logits": route_logits, "w_gate": w_gate, "w_up": w_up, "w_down": w_down}


EPSILON = 1e-06
ROUTE_SCALE = 2.446
ROPE_BASE = 50000.0

def rms_scale(values, gain):
    values = values.astype(jnp.float32)
    mean_square = lax.optimization_barrier(jnp.mean(values * values, axis=-1, keepdims=True))
    return values * lax.rsqrt(mean_square + EPSILON) * gain.astype(jnp.float32)

def rotate(values, positions):
    width = values.shape[-1]
    half = width // 2
    freqs = ROPE_BASE ** (-2.0 * jnp.arange(half, dtype=jnp.float32) / width)
    angles = positions[:, None] * freqs[None, :]
    cosine = jnp.cos(angles)[:, None, :]
    sine = jnp.sin(angles)[:, None, :]
    first = values[..., :half]
    second = values[..., half:]
    return jnp.concatenate([first * cosine - second * sine, second * cosine + first * sine], axis=-1)

def ancestry(parents):
    count = parents.shape[-1]
    nodes = jnp.arange(count, dtype=jnp.int32)
    reach = (parents[:, :, None] == nodes[None, None, :]).astype(jnp.float32) + jnp.eye(count, dtype=jnp.float32)[None]
    for level in range(count.bit_length()):
        reach = jnp.minimum(jnp.einsum('rij,rjk->rik', reach, reach, precision=lax.Precision.HIGHEST), 1.0)
    return reach

def expand(rows, key_up, value_up):
    count = rows.shape[0]
    heads_here = key_up.shape[1] // NOPE
    key_nope = jnp.dot(rows[:, :RANK], key_up, preferred_element_type=jnp.float32).astype(jnp.bfloat16).reshape(count, heads_here, NOPE)
    values = jnp.dot(rows[:, :RANK], value_up, preferred_element_type=jnp.float32).astype(jnp.bfloat16).reshape(count, heads_here, VDIM)
    shared = jnp.broadcast_to(rows[:, None, RANK:], (count, heads_here, ROPE))
    return (jnp.concatenate([key_nope, shared], axis=-1), values)

def reference(hidden_in, attn_gain, w_query, w_latent, kv_gain, w_key_up, w_value_up, w_out, cache_rows, slot_request, slot_block, lengths, parents, accepted, new_slots, moe_gain, routes, route_logits, w_gate, w_up, w_down):
    scale = (NOPE + ROPE) ** (-0.5)
    normed = rms_scale(hidden_in, attn_gain).astype(jnp.bfloat16)
    reach = ancestry(parents)
    depth = lax.optimization_barrier(jnp.sum(reach, axis=-1)) - 1.0
    positions = (lengths.astype(jnp.float32)[:, None] + depth).reshape(TOKENS)
    query_full = jnp.dot(normed, w_query.T, preferred_element_type=jnp.float32).reshape(TOKENS, HEADS, NOPE + ROPE)
    queries = jnp.concatenate([query_full[..., :NOPE], rotate(query_full[..., NOPE:], positions)], axis=-1).astype(jnp.bfloat16)
    compressed = jnp.dot(normed, w_latent.T, preferred_element_type=jnp.float32)
    draft_rows = jnp.concatenate([rms_scale(compressed[:, :RANK], kv_gain), rotate(compressed[:, None, RANK:], positions)[:, 0]], axis=-1).astype(jnp.bfloat16)
    chosen = (jnp.arange(REQS, dtype=jnp.int32)[:, None] * DRAFT + accepted).reshape(-1)
    new_rows = jnp.zeros((NEW_ROWS, RANK + ROPE), jnp.bfloat16).at[new_slots.reshape(-1)].set(draft_rows[chosen])
    cache_keys, cache_values = expand(cache_rows, w_key_up, w_value_up)
    draft_keys, draft_values = expand(draft_rows, w_key_up, w_value_up)
    target = jnp.where(slot_request >= 0, slot_request, REQS)
    table = jnp.zeros((REQS, MAXB), jnp.int32).at[target, slot_block].set(jnp.arange(POOL, dtype=jnp.int32), mode='drop')
    key_offsets = jnp.arange(BLOCK, dtype=jnp.int32)
    key_order = jnp.arange(MAXB * BLOCK, dtype=jnp.int32)

    def attend(request):
        row_ids = (table[request][:, None] * BLOCK + key_offsets[None, :]).reshape(-1)
        keys_here = cache_keys[row_ids].astype(jnp.float32)
        values_here = cache_values[row_ids].astype(jnp.float32)
        live = key_order < lengths[request]
        first = request * DRAFT
        query_here = lax.dynamic_slice_in_dim(queries, first, DRAFT, 0).astype(jnp.float32)
        own_keys = lax.dynamic_slice_in_dim(draft_keys, first, DRAFT, 0).astype(jnp.float32)
        own_values = lax.dynamic_slice_in_dim(draft_values, first, DRAFT, 0).astype(jnp.float32)
        seen = reach[request] > 0.5
        scores = jnp.einsum('qhd,khd->qhk', query_here, keys_here) * scale
        weights = jnp.where(live[None, None, :], jnp.exp(scores), 0.0)
        own_scores = jnp.einsum('qhd,khd->qhk', query_here, own_keys) * scale
        own_weights = jnp.where(seen[:, None, :], jnp.exp(own_scores), 0.0)
        denom = lax.optimization_barrier(jnp.sum(weights, axis=-1)) + lax.optimization_barrier(jnp.sum(own_weights, axis=-1))
        numer = jnp.einsum('qhk,khv->qhv', weights.astype(jnp.bfloat16).astype(jnp.float32), values_here)
        numer = numer + jnp.einsum('qhk,khv->qhv', own_weights.astype(jnp.bfloat16).astype(jnp.float32), own_values)
        return (numer / denom[..., None]).astype(jnp.bfloat16)
    attended = lax.map(attend, jnp.arange(REQS, dtype=jnp.int32))
    attn_sum = jnp.dot(attended.reshape(TOKENS, HEADS * VDIM), w_out, preferred_element_type=jnp.float32)
    resid = (hidden_in.astype(jnp.float32) + attn_sum).astype(jnp.bfloat16)
    moe_in = rms_scale(resid, moe_gain).astype(jnp.bfloat16)
    sigma = jax.nn.sigmoid(route_logits.astype(jnp.float32))
    route_weight = ROUTE_SCALE * sigma / lax.optimization_barrier(jnp.sum(sigma, axis=-1, keepdims=True))
    grouped_routes = routes.reshape(N_BLK, TOK_DEV * TOPK)
    onehot = (grouped_routes[..., None] == jnp.arange(EXPERTS, dtype=jnp.int32)).astype(jnp.int32)
    rank = lax.optimization_barrier(jnp.sum((jnp.cumsum(onehot, axis=1) - onehot) * onehot, axis=-1))
    slot_ids = (jnp.arange(N_BLK, dtype=jnp.int32)[:, None] * CAP + rank).reshape(-1)
    token_of = jnp.arange(TOKENS * TOPK, dtype=jnp.int32) // TOPK
    table_tokens = jnp.full((EXPERTS, N_BLK * CAP), TOKENS, jnp.int32).at[routes.reshape(-1), slot_ids].set(token_of)
    table_weights = jnp.zeros((EXPERTS, N_BLK * CAP), jnp.float32).at[routes.reshape(-1), slot_ids].set(route_weight.reshape(-1))
    moe_pad = jnp.concatenate([moe_in, jnp.zeros((1, D), jnp.bfloat16)], axis=0)

    def expert_step(routed, inputs):
        gate_w, up_w, down_w, token_ids, mixing = inputs
        rows_here = moe_pad[token_ids]
        gate_val = jnp.dot(rows_here, gate_w.T, preferred_element_type=jnp.float32)
        up_val = jnp.dot(rows_here, up_w.T, preferred_element_type=jnp.float32)
        act = (jax.nn.silu(gate_val) * up_val).astype(jnp.bfloat16)
        output = jnp.dot(act, down_w, preferred_element_type=jnp.float32)
        return (routed.at[token_ids].add(mixing[:, None] * output, mode='drop'), jnp.zeros((), jnp.float32))
    routed, unused = lax.scan(expert_step, jnp.zeros((TOKENS, D), jnp.float32), (w_gate, w_up, w_down, table_tokens, table_weights))
    layer_out = (resid.astype(jnp.float32) + routed).astype(jnp.bfloat16)
    return (layer_out, new_rows)
```

```python
import functools

import jax
import jax.numpy as jnp
from jax import lax
from jax.experimental import pallas as pl
from jax.experimental.pallas import tpu as pltpu
from jax.sharding import PartitionSpec as P

NOPE = 128
ROPE = 64
HALF = ROPE // 2
VDIM = 128
RANK = 512
NEW_DEV = 16
LANES = 128

EPSILON = 1e-06
ROUTE_SCALE = 2.446
ROPE_BASE = 50000.0
MIB = 1 << 20

f32 = jnp.float32
bf16 = jnp.bfloat16


def params(mib):
    return pltpu.CompilerParams(vmem_limit_bytes=mib * MIB)


def cost(flops, nbytes, trans=0):
    return pl.CostEstimate(flops=flops, bytes_accessed=nbytes, transcendentals=trans)


def nt(left, right):
    return lax.dot_general(left, right, (((1,), (1,)), ((), ())), preferred_element_type=f32)


def nn(left, right):
    return jnp.dot(left, right, preferred_element_type=f32)


def phases(count):
    out, stride = [], count
    while stride > 1:
        radix = 4 if stride == count and count >= 4 else 2
        stride //= radix
        out.append((radix, stride))
    return out


def swap(value, axis, bit):
    count = lax.axis_size(axis)
    return lax.ppermute(value, axis, [(i, i ^ bit) for i in range(count)])


def gather_blocks(value, count):
    (radix, stride), *rest = phases(count)
    pieces = [jnp.stack([value] + [swap(value, "blk", stride * j) for j in range(1, radix)])]
    for _, stride in rest:
        pieces = pieces + [swap(p, "blk", stride) for p in pieces]
    return pieces


def add16(left, right):
    return (left.astype(f32) + right.astype(f32)).astype(bf16)


def scatter_blocks(pieces, count):
    (radix, stride0), *rest = phases(count)
    for _, stride in reversed(rest):
        half = len(pieces) // 2
        got = [swap(p, "blk", stride) for p in pieces[half:]]
        pieces = [add16(p, g) for p, g in zip(pieces[:half], got)]
    (last,) = pieces
    return [last[0]] + [swap(last[j], "blk", stride0 * j) for j in range(1, radix)]


def place_of(relative, count):
    (radix, stride), *rest = phases(count)
    place = relative // stride
    size = radix
    for _, step in rest:
        place = place + (relative // step) % 2 * size
        size *= 2
    return place


def pre_kernel(
    heads, experts, place_ref, len_ref, hidden_ref, gain_ref, parents_ref, routes_ref, logits_ref,
    query_hbm, latent_hbm, out_ref, latent_ref, trig_ref, reach_ref, wq, wl, sems,
):
    copy_q = pltpu.make_async_copy(query_hbm, wq, sems.at[0])
    copy_l = pltpu.make_async_copy(latent_hbm, wl, sems.at[1])
    copy_q.start()
    copy_l.start()
    tok = hidden_ref.shape[0]
    rows = lax.broadcasted_iota(jnp.int32, (tok, tok), 0)
    cols = lax.broadcasted_iota(jnp.int32, (tok, tok), 1)
    eye = (rows == cols).astype(f32)
    below = jnp.where(rows == parents_ref[...], 1.0, 0.0) + eye
    for _ in range(max(1, (tok - 1).bit_length())):
        step = below.astype(bf16)
        below = jnp.minimum(nn(step, step), 1.0)
    reach = nt(eye.astype(bf16), below.astype(bf16))
    reach_ref[...] = reach
    depth = jnp.sum(reach, axis=-1, keepdims=True) - 1.0
    position = len_ref[place_ref[0]].astype(f32) + depth
    lane = lax.broadcasted_iota(jnp.int32, (1, LANES), 1)
    freqs = ROPE_BASE ** (-2.0 * (lane % HALF).astype(f32) / ROPE)
    angles = position * freqs
    cosine, sine = jnp.cos(angles), jnp.sin(angles)
    trig_ref[:, :LANES] = cosine
    trig_ref[:, LANES:] = sine
    sigma = jax.nn.sigmoid(logits_ref[...])
    weight = ROUTE_SCALE * sigma / jnp.sum(sigma, axis=-1, keepdims=True)
    mix = jnp.zeros((tok, LANES), f32)
    for k in range(weight.shape[1]):
        mix = mix + jnp.where(lane % experts == routes_ref[:, k : k + 1], weight[:, k : k + 1], 0.0)
    high = mix.astype(bf16).astype(f32)
    mix = jnp.where(lane < experts, high, jnp.where(lane < 2 * experts, mix - high, 0.0))
    hidden = hidden_ref[...].astype(f32)
    mean_square = jnp.mean(hidden * hidden, axis=-1, keepdims=True)
    normed = (hidden * lax.rsqrt(mean_square + EPSILON) * gain_ref[...]).astype(bf16)
    copy_q.wait()
    size = NOPE + ROPE
    for h in range(heads):
        part = nt(normed, wq[h * size : h * size + NOPE])
        out_ref[:, h * NOPE : (h + 1) * NOPE] = part.astype(bf16)
    pad = [jnp.zeros((LANES - heads * HALF, wq.shape[1]), bf16)] if heads * HALF < LANES else []
    first, second = (
        nt(normed, jnp.concatenate(
            [wq[h * size + NOPE + at : h * size + NOPE + at + HALF] for h in range(heads)] + pad))
        for at in (0, HALF)
    )
    base = heads * NOPE
    out_ref[:, base : base + LANES] = (first * cosine - second * sine).astype(bf16)
    out_ref[:, base + LANES : base + 2 * LANES] = (second * cosine + first * sine).astype(bf16)
    out_ref[:, base + 2 * LANES :] = mix.astype(bf16)
    copy_l.wait()
    latent_ref[...] = nt(normed, wl[...])


def prepare(place, lengths, hidden, gain, parents, routes, logits, w_query, w_latent, heads, experts):
    tok, width = hidden.shape
    smem = pl.BlockSpec(memory_space=pltpu.SMEM)
    vmem = pl.BlockSpec(memory_space=pltpu.VMEM)
    anyw = pl.BlockSpec(memory_space=pl.ANY)
    lanes = heads * NOPE + 3 * LANES
    return pl.pallas_call(
        functools.partial(pre_kernel, heads, experts),
        out_shape=(
            jax.ShapeDtypeStruct((tok, lanes), bf16),
            jax.ShapeDtypeStruct((tok, w_latent.shape[0]), f32),
            jax.ShapeDtypeStruct((tok, 2 * LANES), f32),
            jax.ShapeDtypeStruct((tok, tok), f32),
        ),
        in_specs=[smem, smem, vmem, vmem, vmem, vmem, vmem, anyw, anyw],
        out_specs=(vmem,) * 4,
        scratch_shapes=[
            pltpu.VMEM(w_query.shape, bf16),
            pltpu.VMEM(w_latent.shape, bf16),
            pltpu.SemaphoreType.DMA((2,)),
        ],
        compiler_params=params(24),
        cost_estimate=cost(2 * tok * width * 1100, 2 * width * 1100),
        name="prepare",
    )(place, lengths, hidden, gain[None], parents, routes, logits, w_query, w_latent)


def spread(heads):
    row = lax.broadcasted_iota(jnp.int32, (ROPE, 2 * LANES), 0)
    col = lax.broadcasted_iota(jnp.int32, (ROPE, 2 * LANES), 1)
    inside = col % LANES < heads * HALF
    return jnp.where((row == col // LANES * HALF + col % HALF) & inside, 1.0, 0.0).astype(bf16)


def keys_values(rows, key_up, value_up, heads):
    low = rows[:, :RANK]
    nope = nn(low, key_up).astype(bf16)
    rope = nn(rows[:, RANK:], spread(heads)).astype(bf16)
    return jnp.concatenate([nope, rope], axis=-1), nn(low, value_up).astype(bf16)


def expand_kernel(heads, rows_ref, key_ref, value_ref, keys_out, values_out):
    keys_out[...], values_out[...] = keys_values(rows_ref[...], key_ref[...], value_ref[...], heads)


def expand(rows, key_up, value_up, heads):
    vmem = pl.BlockSpec(memory_space=pltpu.VMEM)
    count = rows.shape[0]
    return pl.pallas_call(
        functools.partial(expand_kernel, heads),
        out_shape=(
            jax.ShapeDtypeStruct((count, heads * NOPE + 2 * LANES), bf16),
            jax.ShapeDtypeStruct((count, heads * VDIM), bf16),
        ),
        in_specs=[vmem] * 3,
        out_specs=(vmem,) * 2,
        compiler_params=params(16),
        cost_estimate=cost(4 * count * RANK * heads * NOPE, 4 * count * RANK),
        name="expand",
    )(rows, key_up, value_up)


def by_head(query, heads):
    tok, lanes = query.shape[0], heads * NOPE + 2 * LANES
    lane = lax.broadcasted_iota(jnp.int32, (1, lanes), 1)
    head = jnp.where(lane < heads * NOPE, lane // NOPE, lane % LANES // HALF)
    query = query[:, :lanes].astype(f32)
    return jnp.concatenate(
        [jnp.where(head == h, query, 0.0) for h in range(heads)], axis=0
    ).astype(bf16)


def attend(query, keys, values, seen, heads):
    tok = query.shape[0] // heads
    scale = (NOPE + ROPE) ** (-0.5)
    weight = jnp.where(seen, jnp.exp(nt(query, keys) * scale), 0.0)
    high = weight.astype(bf16)
    low = (weight - high.astype(f32)).astype(bf16)
    full = nn(high, values)
    numer = jnp.concatenate(
        [full[h * tok : (h + 1) * tok, h * VDIM : (h + 1) * VDIM] for h in range(heads)], axis=0
    )
    ones = jnp.ones((16, keys.shape[0]), bf16)
    denom = nt(ones, high) + nt(ones, low)
    if denom.shape[1] < LANES:
        denom = jnp.concatenate([denom, jnp.zeros((16, LANES - denom.shape[1]), f32)], axis=-1)
    return jnp.concatenate([numer, denom], axis=0)


def slots_kernel(heads, slots, block, pieces, place_ref, live_ref, keys_ref, values_ref, *refs):
    queries, outs = refs[:pieces], refs[pieces:]
    each = queries[0].shape[0]
    for out in outs:
        out[...] = jnp.zeros(out.shape, out.dtype)
    parts = []
    lane = lax.broadcasted_iota(jnp.int32, (1, block), 1)
    for s in range(slots):
        place = place_ref[s]
        query = queries[0][place % each]
        for p in range(1, pieces):
            query = jnp.where(place // each == p, queries[p][place % each], query)
        keys, values = (r[s * block : (s + 1) * block] for r in (keys_ref, values_ref))
        parts.append(attend(by_head(query, heads), keys, values, lane < live_ref[s], heads))
    for s in range(slots):
        place = place_ref[s]
        total = parts[s]
        for other in range(slots):
            if other != s:
                total = total + jnp.where(place_ref[other] == place, parts[other], 0.0)
        for p, out in enumerate(outs):
            @pl.when(place // each == p)
            def _():
                out[place % each] = total.astype(bf16)


def attend_slots(place, live, keys, values, queries, heads, block):
    smem = pl.BlockSpec(memory_space=pltpu.SMEM)
    vmem = pl.BlockSpec(memory_space=pltpu.VMEM)
    slots, each, tok = place.shape[0], queries[0].shape[0], queries[0].shape[1]
    out = jax.ShapeDtypeStruct((each, heads * tok + 16, LANES), bf16)
    return pl.pallas_call(
        functools.partial(slots_kernel, heads, slots, block, len(queries)),
        out_shape=(out,) * len(queries),
        in_specs=[smem, smem, vmem, vmem] + [vmem] * len(queries),
        out_specs=(vmem,) * len(queries),
        compiler_params=params(24),
        cost_estimate=cost(1 << 28, 2 << 20),
        name="attend_slots",
    )(place, live, keys, values, *queries)


def own_kernel(heads, rows_ref, query_ref, reach_ref, key_ref, value_ref, out_ref):
    keys, values = keys_values(rows_ref[...], key_ref[...], value_ref[...], heads)
    seen = jnp.concatenate([reach_ref[...]] * heads, axis=0) > 0.5
    out_ref[...] = attend(by_head(query_ref[...], heads), keys, values, seen, heads)


def attend_own(rows, query, reach, key_up, value_up, heads):
    vmem = pl.BlockSpec(memory_space=pltpu.VMEM)
    return pl.pallas_call(
        functools.partial(own_kernel, heads),
        out_shape=jax.ShapeDtypeStruct((heads * rows.shape[0] + 16, LANES), f32),
        in_specs=[vmem] * 5,
        out_specs=vmem,
        compiler_params=params(16),
        cost_estimate=cost(1 << 26, 2 << 20),
        name="attend_own",
    )(rows, query, reach, key_up, value_up)


def project_kernel(heads, parts, w_ref, own_ref, *refs):
    total = own_ref[...]
    for ref in refs[:parts]:
        total = total + ref[...].astype(f32)
    count = heads * (total.shape[0] - 16) // heads
    tok = count // heads
    row = lax.broadcasted_iota(jnp.int32, (count, LANES), 0)
    col = lax.broadcasted_iota(jnp.int32, (count, LANES), 1)
    denom = jnp.sum(jnp.where(row == col, total[count : count + 1], 0.0), axis=-1, keepdims=True)
    attended = (total[:count] / denom).astype(bf16)
    wide = jnp.concatenate([attended[h * tok : (h + 1) * tok] for h in range(heads)], axis=-1)
    refs[parts][...] = nn(wide, w_ref[...]).astype(bf16)


def project_out(w_out, own, parts, heads, tok):
    vmem = pl.BlockSpec(memory_space=pltpu.VMEM)
    return pl.pallas_call(
        functools.partial(project_kernel, heads, len(parts)),
        out_shape=jax.ShapeDtypeStruct((tok, w_out.shape[1]), bf16),
        in_specs=[vmem] * (2 + len(parts)),
        out_specs=vmem,
        compiler_params=params(16),
        cost_estimate=cost(2 * tok * w_out.size, 2 * w_out.size),
        name="project_out",
    )(w_out, own, *parts)


def norm_kernel(hidden_ref, mine_ref, other_ref, gain_ref, resid_ref, out_ref):
    added = mine_ref[...].astype(f32) + other_ref[...].astype(f32)
    resid = (hidden_ref[...].astype(f32) + added).astype(bf16)
    resid_ref[...] = resid
    value = resid.astype(f32)
    mean_square = jnp.mean(value * value, axis=-1, keepdims=True)
    out_ref[...] = (value * lax.rsqrt(mean_square + EPSILON) * gain_ref[...]).astype(bf16)


def norm(hidden, mine, other, gain):
    out = jax.ShapeDtypeStruct(hidden.shape, bf16)
    vmem = pl.BlockSpec(memory_space=pltpu.VMEM)
    return pl.pallas_call(
        norm_kernel, out_shape=(out, out), in_specs=[vmem] * 4, out_specs=(vmem, vmem),
        compiler_params=params(16), name="norm",
    )(hidden, mine, other, gain[None])


def expert_kernel(
    experts, index_ref, low_ref, high_ref, mix_low, mix_high, gate_hbm, up_hbm, down_hbm,
    out_low, out_high, gate, up, down, sems,
):
    copies = [
        pltpu.make_async_copy(src.at[0], dst, sems.at[i])
        for i, (src, dst) in enumerate(((gate_hbm, gate), (up_hbm, up), (down_hbm, down)))
    ]
    for copy in copies:
        copy.start()
    each, tok, width = low_ref.shape
    rows = jnp.concatenate(
        [r[...].reshape(each * tok, width) for r in (low_ref, high_ref)], axis=0
    )
    mix = jnp.concatenate(
        [r[...].reshape(each * tok, LANES) for r in (mix_low, mix_high)], axis=0
    ).astype(f32)
    lane = lax.broadcasted_iota(jnp.int32, (1, LANES), 1)
    index = index_ref[0]
    mine = (lane == index) | (lane == index + experts)
    weight = jnp.sum(jnp.where(mine, mix, 0.0), axis=-1, keepdims=True)
    copies[0].wait()
    gated = nt(rows, gate[...])
    gated = gated / (1.0 + jnp.exp(-gated))
    copies[1].wait()
    act = (gated * nt(rows, up[...])).astype(bf16)
    copies[2].wait()
    out = (nn(act, down[...]) * weight).astype(bf16)
    out_low[...] = out[: each * tok].reshape(each, tok, width)
    out_high[...] = out[each * tok :].reshape(each, tok, width)


def expert(index, low, high, mix_low, mix_high, w_gate, w_up, w_down, experts):
    smem = pl.BlockSpec(memory_space=pltpu.SMEM)
    vmem = pl.BlockSpec(memory_space=pltpu.VMEM)
    anyw = pl.BlockSpec(memory_space=pl.ANY)
    each, tok, _ = low.shape
    last = mix_low.shape[-1] // LANES - 1
    mixed = pl.BlockSpec((each, tok, LANES), lambda i: (0, 0, last))
    out = jax.ShapeDtypeStruct(low.shape, bf16)
    whole = pl.BlockSpec(low.shape, lambda i: (0, 0, 0))
    return pl.pallas_call(
        functools.partial(expert_kernel, experts),
        grid=(1,),
        out_shape=(out, out),
        in_specs=[smem, whole, whole, mixed, mixed, anyw, anyw, anyw],
        out_specs=(whole, whole),
        scratch_shapes=[pltpu.VMEM(w.shape[1:], bf16) for w in (w_gate, w_up, w_down)]
        + [pltpu.SemaphoreType.DMA((3,))],
        compiler_params=params(40),
        cost_estimate=cost(12 * each * tok * w_gate.size, 6 * w_gate.size),
        name="expert",
    )(index, low, high, mix_low, mix_high, w_gate, w_up, w_down)


def sum_heads(value):
    count, bit = lax.axis_size("head"), 1
    other = swap(value, "head", bit)
    while 2 * bit < count:
        bit *= 2
        value = add16(value, other)
        other = swap(value, "head", bit)
    return value, other


def join_heads(value):
    if lax.axis_size("head") == 2:
        other = swap(value, "head", 1)
        first = lax.axis_index("head") == 0
        parts = [jnp.where(first, value, other), jnp.where(first, other, value)]
        return jnp.concatenate(parts, axis=1)
    return lax.all_gather(value, "head", axis=1, tiled=True)


def shards(
    hidden_in, attn_gain, w_query, w_latent, kv_gain, w_key_up, w_value_up, w_out, cache_rows,
    slot_request, slot_block, lengths, parents, accepted, new_slots, moe_gain, routes,
    route_logits, w_gate, w_up, w_down,
):
    count = lax.axis_size("blk")
    me = lax.axis_index("blk").astype(jnp.int32)
    tok = hidden_in.shape[0]
    heads = w_key_up.shape[1] // NOPE
    experts = w_gate.shape[0] * count
    index = me[None]
    payload, latent, trig, reach = prepare(
        index, lengths, hidden_in, attn_gain, parents, routes, route_logits, w_query, w_latent,
        heads, experts,
    )
    queries = gather_blocks(payload, count)

    compressed = join_heads(latent)
    low = compressed[:, :RANK]
    low = low * lax.rsqrt(jnp.mean(low * low, axis=-1, keepdims=True) + EPSILON) * kv_gain
    first, second = compressed[:, RANK : RANK + HALF], compressed[:, RANK + HALF :]
    cosine, sine = trig[:, :HALF], trig[:, LANES : LANES + HALF]
    draft_rows = jnp.concatenate(
        [low, first * cosine - second * sine, second * cosine + first * sine], axis=-1
    ).astype(bf16)

    keys, values = expand(cache_rows, w_key_up, w_value_up, heads)
    slots = slot_request.shape[0]
    block = cache_rows.shape[0] // slots
    owner = jnp.maximum(slot_request, 0)
    owner_length = jnp.sum(
        jnp.where(owner[:, None] == jnp.arange(lengths.shape[0])[None, :], lengths[None, :], 0), axis=1
    )
    live = jnp.where(slot_request >= 0, owner_length - slot_block * block, 0)
    place = place_of(owner ^ me, count)
    partial = attend_slots(place, live, keys, values, queries, heads, block)
    parts = scatter_blocks(list(partial), count)
    own = attend_own(draft_rows, payload, reach, w_key_up, w_value_up, heads)
    mine, other = sum_heads(project_out(w_out, own, parts, heads, tok))
    resid, moe_in = norm(hidden_in, mine, other, moe_gain)

    node = jnp.arange(tok, dtype=jnp.int32)
    pick = (accepted.reshape(-1)[:, None] == node[None, :]).astype(bf16)
    chosen = jnp.dot(pick, draft_rows, preferred_element_type=f32).astype(bf16)
    target = new_slots.reshape(-1, 1)
    tail = jnp.concatenate([target // 256, target % 256], axis=1).astype(bf16)
    sent = jnp.concatenate(
        [chosen, tail, jnp.zeros((chosen.shape[0], LANES - ROPE - 2), bf16)], axis=1
    )
    rows = jnp.concatenate(gather_blocks(sent, count)).reshape(-1, sent.shape[1])
    at = RANK + ROPE
    slot = rows[:, at].astype(f32) * 256.0 + rows[:, at + 1].astype(f32)
    here = (me * NEW_DEV + jnp.arange(NEW_DEV, dtype=jnp.int32)).astype(f32)
    new_rows = jnp.dot(
        (here[:, None] == slot[None, :]).astype(bf16), rows[:, :at], preferred_element_type=f32
    ).astype(bf16)

    tokens = gather_blocks(moe_in, count)
    half = len(tokens) // 2
    outs = [
        expert(index, tokens[i], tokens[i + half], queries[i], queries[i + half],
               w_gate, w_up, w_down, experts)
        for i in range(half)
    ]
    back = scatter_blocks([o[0] for o in outs] + [o[1] for o in outs], count)
    total = back[0].astype(f32)
    for value in back[1:]:
        total = total + value.astype(f32)
    mine, other = sum_heads(total.astype(bf16))
    routed = mine.astype(f32) + other.astype(f32)
    layer_out = (resid.astype(f32) + routed).astype(bf16)
    return (layer_out, new_rows)


def solution(mesh):
    return jax.shard_map(
        shards,
        mesh=mesh,
        in_specs=(
            P("blk", None),
            P(),
            P("head", None),
            P("head", None),
            P(),
            P(None, "head"),
            P(None, "head"),
            P("head", None),
            P("blk", None),
            P("blk"),
            P("blk"),
            P(),
            P("blk", None),
            P("blk", None),
            P("blk", None),
            P(),
            P("blk", None),
            P("blk", None),
            P("blk", "head", None),
            P("blk", "head", None),
            P("blk", "head", None),
        ),
        out_specs=(P("blk", None), P("blk", None)),
        check_vma=False,
    )
```

```python
import functools

import jax
import jax.numpy as jnp
from jax import lax
from jax.experimental import pallas as pl
from jax.experimental.pallas import tpu as pltpu
from jax.sharding import PartitionSpec as P

NOPE = 128
ROPE = 64
HALF = ROPE // 2
VDIM = 128
RANK = 512
NEW_DEV = 16
LANES = 128

EPSILON = 1e-06
ROUTE_SCALE = 2.446
ROPE_BASE = 50000.0
MIB = 1 << 20

f32 = jnp.float32
bf16 = jnp.bfloat16


def params(mib):
    return pltpu.CompilerParams(vmem_limit_bytes=mib * MIB)


def cost(flops, nbytes, trans=0):
    return pl.CostEstimate(flops=flops, bytes_accessed=nbytes, transcendentals=trans)


def nt(left, right):
    return lax.dot_general(left, right, (((1,), (1,)), ((), ())), preferred_element_type=f32)


def nn(left, right):
    return jnp.dot(left, right, preferred_element_type=f32)


def phases(count):
    out, stride = [], count
    while stride > 1:
        radix = 4 if stride == count and count >= 4 else 2
        stride //= radix
        out.append((radix, stride))
    return out


def swap(value, axis, bit):
    count = lax.axis_size(axis)
    return lax.ppermute(value, axis, [(i, i ^ bit) for i in range(count)])


def gather_blocks(value, count):
    (radix, stride), *rest = phases(count)
    pieces = [jnp.stack([value] + [swap(value, "blk", stride * j) for j in range(1, radix)])]
    for _, stride in rest:
        pieces = pieces + [swap(p, "blk", stride) for p in pieces]
    return pieces


def add16(left, right):
    return (left.astype(f32) + right.astype(f32)).astype(bf16)


def scatter_blocks(pieces, count, done=0):
    (radix, stride0), *rest = phases(count)
    for _, stride in reversed(rest):
        if stride == done:
            continue
        half = len(pieces) // 2
        got = [swap(p, "blk", stride) for p in pieces[half:]]
        pieces = [add16(p, g) for p, g in zip(pieces[:half], got)]
    (last,) = pieces
    return [last[0]] + [swap(last[j], "blk", stride0 * j) for j in range(1, radix)]


def place_of(relative, count):
    (radix, stride), *rest = phases(count)
    place = relative // stride
    size = radix
    for _, step in rest:
        place = place + (relative // step) % 2 * size
        size *= 2
    return place


def pre_kernel(
    heads, experts, place_ref, len_ref, hidden_ref, gain_ref, parents_ref, routes_ref, logits_ref,
    query_hbm, latent_hbm, out_ref, latent_ref, trig_ref, reach_ref, wq, wl, sems,
):
    copy_q = pltpu.make_async_copy(query_hbm, wq, sems.at[0])
    copy_l = pltpu.make_async_copy(latent_hbm, wl, sems.at[1])
    copy_q.start()
    copy_l.start()
    tok = hidden_ref.shape[0]
    rows = lax.broadcasted_iota(jnp.int32, (tok, tok), 0)
    cols = lax.broadcasted_iota(jnp.int32, (tok, tok), 1)
    eye = (rows == cols).astype(f32)
    below = jnp.where(rows == parents_ref[...], 1.0, 0.0) + eye
    for _ in range(max(1, (tok - 1).bit_length())):
        step = below.astype(bf16)
        below = jnp.minimum(nn(step, step), 1.0)
    reach = nt(eye.astype(bf16), below.astype(bf16))
    reach_ref[...] = reach
    depth = jnp.sum(reach, axis=-1, keepdims=True) - 1.0
    position = len_ref[place_ref[0]].astype(f32) + depth
    lane = lax.broadcasted_iota(jnp.int32, (1, LANES), 1)
    freqs = ROPE_BASE ** (-2.0 * (lane % HALF).astype(f32) / ROPE)
    angles = position * freqs
    cosine, sine = jnp.cos(angles), jnp.sin(angles)
    trig_ref[:, :LANES] = cosine
    trig_ref[:, LANES:] = sine
    sigma = jax.nn.sigmoid(logits_ref[...])
    weight = ROUTE_SCALE * sigma / jnp.sum(sigma, axis=0, keepdims=True)
    named = lax.broadcasted_iota(jnp.int32, (LANES, 1), 0)
    mix = jnp.zeros((LANES, tok), f32)
    for k in range(weight.shape[0]):
        mix = mix + jnp.where(named % experts == routes_ref[k : k + 1], weight[k : k + 1], 0.0)
    high = mix.astype(bf16).astype(f32)
    mix = jnp.where(named < experts, high, jnp.where(named < 2 * experts, mix - high, 0.0))
    mix = nt(eye.astype(bf16), mix.astype(bf16))
    hidden = hidden_ref[...].astype(f32)
    mean_square = jnp.mean(hidden * hidden, axis=-1, keepdims=True)
    normed = (hidden * lax.rsqrt(mean_square + EPSILON) * gain_ref[...]).astype(bf16)
    copy_q.wait()
    size = NOPE + ROPE
    for h in range(heads):
        part = nt(normed, wq[h * size : h * size + NOPE])
        out_ref[:, h * NOPE : (h + 1) * NOPE] = part.astype(bf16)
    pad = [jnp.zeros((LANES - heads * HALF, wq.shape[1]), bf16)] if heads * HALF < LANES else []
    first, second = (
        nt(normed, jnp.concatenate(
            [wq[h * size + NOPE + at : h * size + NOPE + at + HALF] for h in range(heads)] + pad))
        for at in (0, HALF)
    )
    base = heads * NOPE
    out_ref[:, base : base + LANES] = (first * cosine - second * sine).astype(bf16)
    out_ref[:, base + LANES : base + 2 * LANES] = (second * cosine + first * sine).astype(bf16)
    out_ref[:, base + 2 * LANES :] = mix.astype(bf16)
    copy_l.wait()
    latent_ref[...] = nt(normed, wl[...])


def prepare(place, lengths, hidden, gain, parents, routes, logits, w_query, w_latent, heads, experts):
    tok, width = hidden.shape
    smem = pl.BlockSpec(memory_space=pltpu.SMEM)
    hbm = pl.BlockSpec(memory_space=pltpu.HBM)
    lanes = heads * NOPE + 3 * LANES
    small = (hidden, gain[None], parents, routes.T, logits.T)
    whole = lambda shape: pl.BlockSpec(shape, lambda i: (0,) * len(shape))
    return pl.pallas_call(
        functools.partial(pre_kernel, heads, experts),
        grid=(1,),
        out_shape=(
            jax.ShapeDtypeStruct((tok, lanes), bf16),
            jax.ShapeDtypeStruct((tok, w_latent.shape[0]), f32),
            jax.ShapeDtypeStruct((tok, 2 * LANES), f32),
            jax.ShapeDtypeStruct((tok, tok), f32),
        ),
        in_specs=[smem, smem, *(whole(v.shape) for v in small), hbm, hbm],
        out_specs=tuple(
            whole(shape)
            for shape in ((tok, lanes), (tok, w_latent.shape[0]), (tok, 2 * LANES), (tok, tok))
        ),
        scratch_shapes=[
            pltpu.VMEM(w_query.shape, bf16),
            pltpu.VMEM(w_latent.shape, bf16),
            pltpu.SemaphoreType.DMA((2,)),
        ],
        compiler_params=params(56),
        cost_estimate=cost(2 * tok * width * 1100, 2 * width * 1100),
        name="prepare",
    )(place, lengths, *small, w_query, w_latent)


def spread(heads):
    row = lax.broadcasted_iota(jnp.int32, (ROPE, 2 * LANES), 0)
    col = lax.broadcasted_iota(jnp.int32, (ROPE, 2 * LANES), 1)
    inside = col % LANES < heads * HALF
    return jnp.where((row == col // LANES * HALF + col % HALF) & inside, 1.0, 0.0).astype(bf16)


def keys_values(rows, key_up, value_up, heads):
    low = rows[:, :RANK]
    nope = nn(low, key_up).astype(bf16)
    rope = nn(rows[:, RANK:], spread(heads)).astype(bf16)
    return jnp.concatenate([nope, rope], axis=-1), nn(low, value_up).astype(bf16)


def expand_kernel(heads, rows_ref, key_ref, value_ref, keys_out, values_out):
    keys_out[...], values_out[...] = keys_values(rows_ref[...], key_ref[...], value_ref[...], heads)


def expand(rows, key_up, value_up, heads):
    vmem = pl.BlockSpec(memory_space=pltpu.VMEM)
    count = rows.shape[0]
    return pl.pallas_call(
        functools.partial(expand_kernel, heads),
        out_shape=(
            jax.ShapeDtypeStruct((count, heads * NOPE + 2 * LANES), bf16),
            jax.ShapeDtypeStruct((count, heads * VDIM), bf16),
        ),
        in_specs=[vmem] * 3,
        out_specs=(vmem,) * 2,
        compiler_params=params(16),
        cost_estimate=cost(4 * count * RANK * heads * NOPE, 4 * count * RANK),
        name="expand",
    )(rows, key_up, value_up)


def by_head(query, heads):
    tok, lanes = query.shape[0], heads * NOPE + 2 * LANES
    lane = lax.broadcasted_iota(jnp.int32, (1, lanes), 1)
    head = jnp.where(lane < heads * NOPE, lane // NOPE, lane % LANES // HALF)
    query = query[:, :lanes].astype(f32)
    return jnp.concatenate(
        [jnp.where(head == h, query, 0.0) for h in range(heads)], axis=0
    ).astype(bf16)


def attend(query, keys, values, seen, heads):
    tok = query.shape[0] // heads
    scale = (NOPE + ROPE) ** (-0.5)
    weight = jnp.where(seen, jnp.exp(nt(query, keys) * scale), 0.0)
    high = weight.astype(bf16)
    low = (weight - high.astype(f32)).astype(bf16)
    full = nn(high, values)
    numer = jnp.concatenate(
        [full[h * tok : (h + 1) * tok, h * VDIM : (h + 1) * VDIM] for h in range(heads)], axis=0
    )
    ones = jnp.ones((16, keys.shape[0]), bf16)
    denom = nt(ones, high) + nt(ones, low)
    if denom.shape[1] < LANES:
        denom = jnp.concatenate([denom, jnp.zeros((16, LANES - denom.shape[1]), f32)], axis=-1)
    return jnp.concatenate([numer, denom], axis=0)


def slots_kernel(
    heads, slots, block, pieces, experts, place_ref, live_ref, index_ref, keys_ref, values_ref, *refs
):
    queries, outs, mixes = refs[:pieces], refs[pieces : 2 * pieces], refs[2 * pieces :]
    each, tok, lanes = queries[0].shape
    named = lax.broadcasted_iota(jnp.int32, (1, LANES), 1)
    mine = (named == index_ref[0]) | (named == index_ref[0] + experts)
    for query, mix in zip(queries, mixes):
        shares = query[:, :, lanes - LANES :].reshape(each * tok, LANES).astype(f32)
        mix[...] = jnp.sum(jnp.where(mine, shares, 0.0), axis=-1, keepdims=True)
    for out in outs:
        out[...] = jnp.zeros(out.shape, out.dtype)
    parts = []
    lane = lax.broadcasted_iota(jnp.int32, (1, block), 1)
    for s in range(slots):
        place = place_ref[s]
        query = queries[0][place % each]
        for p in range(1, pieces):
            query = jnp.where(place // each == p, queries[p][place % each], query)
        keys, values = (r[s * block : (s + 1) * block] for r in (keys_ref, values_ref))
        parts.append(attend(by_head(query, heads), keys, values, lane < live_ref[s], heads))
    for s in range(slots):
        place = place_ref[s]
        total = parts[s]
        for other in range(slots):
            if other != s:
                total = total + jnp.where(place_ref[other] == place, parts[other], 0.0)
        for p, out in enumerate(outs):
            @pl.when(place // each == p)
            def _():
                out[place % each] = total.astype(bf16)


def attend_slots(place, live, index, keys, values, queries, heads, block, experts):
    smem = pl.BlockSpec(memory_space=pltpu.SMEM)
    vmem = pl.BlockSpec(memory_space=pltpu.VMEM)
    slots, each, tok = place.shape[0], queries[0].shape[0], queries[0].shape[1]
    pieces = len(queries)
    out = jax.ShapeDtypeStruct((each, heads * tok + 16, LANES), bf16)
    mix = jax.ShapeDtypeStruct((each * tok, 1), f32)
    results = pl.pallas_call(
        functools.partial(slots_kernel, heads, slots, block, pieces, experts),
        out_shape=(out,) * pieces + (mix,) * pieces,
        in_specs=[smem, smem, smem, vmem, vmem] + [vmem] * pieces,
        out_specs=(vmem,) * (2 * pieces),
        compiler_params=params(24),
        cost_estimate=cost(1 << 28, 2 << 20),
        name="attend_slots",
    )(place, live, index, keys, values, *queries)
    return list(results[:pieces]), results[pieces:]


def own_kernel(heads, rows_ref, query_ref, reach_ref, key_ref, value_ref, out_ref):
    keys, values = keys_values(rows_ref[...], key_ref[...], value_ref[...], heads)
    seen = jnp.concatenate([reach_ref[...]] * heads, axis=0) > 0.5
    out_ref[...] = attend(by_head(query_ref[...], heads), keys, values, seen, heads)


def attend_own(rows, query, reach, key_up, value_up, heads):
    vmem = pl.BlockSpec(memory_space=pltpu.VMEM)
    return pl.pallas_call(
        functools.partial(own_kernel, heads),
        out_shape=jax.ShapeDtypeStruct((heads * rows.shape[0] + 16, LANES), f32),
        in_specs=[vmem] * 5,
        out_specs=vmem,
        compiler_params=params(16),
        cost_estimate=cost(1 << 26, 2 << 20),
        name="attend_own",
    )(rows, query, reach, key_up, value_up)


def project_kernel(heads, parts, w_ref, own_ref, *refs):
    total = own_ref[...]
    for ref in refs[:parts]:
        total = total + ref[...].astype(f32)
    count = heads * (total.shape[0] - 16) // heads
    tok = count // heads
    row = lax.broadcasted_iota(jnp.int32, (count, LANES), 0)
    col = lax.broadcasted_iota(jnp.int32, (count, LANES), 1)
    denom = jnp.sum(jnp.where(row == col, total[count : count + 1], 0.0), axis=-1, keepdims=True)
    attended = (total[:count] / denom).astype(bf16)
    wide = jnp.concatenate([attended[h * tok : (h + 1) * tok] for h in range(heads)], axis=-1)
    refs[parts][...] = nn(wide, w_ref[...]).astype(bf16)


def project_out(w_out, own, parts, heads, tok):
    vmem = pl.BlockSpec(memory_space=pltpu.VMEM)
    return pl.pallas_call(
        functools.partial(project_kernel, heads, len(parts)),
        out_shape=jax.ShapeDtypeStruct((tok, w_out.shape[1]), bf16),
        in_specs=[vmem] * (2 + len(parts)),
        out_specs=vmem,
        compiler_params=params(16),
        cost_estimate=cost(2 * tok * w_out.size, 2 * w_out.size),
        name="project_out",
    )(w_out, own, *parts)


def norm_kernel(hidden_ref, mine_ref, other_ref, gain_ref, resid_ref, out_ref):
    added = mine_ref[...].astype(f32) + other_ref[...].astype(f32)
    resid = (hidden_ref[...].astype(f32) + added).astype(bf16)
    resid_ref[...] = resid
    value = resid.astype(f32)
    mean_square = jnp.mean(value * value, axis=-1, keepdims=True)
    out_ref[...] = (value * lax.rsqrt(mean_square + EPSILON) * gain_ref[...]).astype(bf16)


def norm(hidden, mine, other, gain):
    out = jax.ShapeDtypeStruct(hidden.shape, bf16)
    vmem = pl.BlockSpec(memory_space=pltpu.VMEM)
    return pl.pallas_call(
        norm_kernel, out_shape=(out, out), in_specs=[vmem] * 4, out_specs=(vmem, vmem),
        compiler_params=params(16), name="norm",
    )(hidden, mine, other, gain[None])


def expert_kernel(
    low_ref, high_ref, mix_low, mix_high, gate_hbm, up_hbm, down_hbm, out_low, out_high,
    gate, up, down, sems,
):
    copies = [
        pltpu.make_async_copy(src.at[0], dst, sems.at[i])
        for i, (src, dst) in enumerate(((gate_hbm, gate), (up_hbm, up), (down_hbm, down)))
    ]
    for copy in copies:
        copy.start()
    each, tok, width = low_ref.shape
    rows = jnp.concatenate(
        [r[...].reshape(each * tok, width) for r in (low_ref, high_ref)], axis=0
    )
    weight = jnp.concatenate([mix_low[...], mix_high[...]], axis=0)
    copies[0].wait()
    gated = nt(rows, gate[...])
    gated = gated / (1.0 + jnp.exp(-gated))
    copies[1].wait()
    act = (gated * nt(rows, up[...])).astype(bf16)
    copies[2].wait()
    out = (nn(act, down[...]) * weight).astype(bf16)
    out_low[...] = out[: each * tok].reshape(each, tok, width)
    out_high[...] = out[each * tok :].reshape(each, tok, width)


def expert(low, high, mix_low, mix_high, w_gate, w_up, w_down):
    vmem = pl.BlockSpec(memory_space=pltpu.VMEM)
    hbm = pl.BlockSpec(memory_space=pltpu.HBM)
    each, tok, _ = low.shape
    out = jax.ShapeDtypeStruct(low.shape, bf16)
    return pl.pallas_call(
        expert_kernel,
        out_shape=(out, out),
        in_specs=[vmem] * 4 + [hbm] * 3,
        out_specs=(vmem, vmem),
        scratch_shapes=[pltpu.VMEM(w.shape[1:], bf16) for w in (w_gate, w_up, w_down)]
        + [pltpu.SemaphoreType.DMA((3,))],
        compiler_params=params(28),
        cost_estimate=cost(12 * each * tok * w_gate.size, 6 * w_gate.size),
        name="expert",
    )(low, high, mix_low, mix_high, w_gate, w_up, w_down)


def sum_heads(value):
    count, bit = lax.axis_size("head"), 1
    other = swap(value, "head", bit)
    while 2 * bit < count:
        bit *= 2
        value = add16(value, other)
        other = swap(value, "head", bit)
    return value, other


def join_heads(value):
    if lax.axis_size("head") == 2:
        other = swap(value, "head", 1)
        first = lax.axis_index("head") == 0
        parts = [jnp.where(first, value, other), jnp.where(first, other, value)]
        return jnp.concatenate(parts, axis=1)
    return lax.all_gather(value, "head", axis=1, tiled=True)


def shards(
    hidden_in, attn_gain, w_query, w_latent, kv_gain, w_key_up, w_value_up, w_out, cache_rows,
    slot_request, slot_block, lengths, parents, accepted, new_slots, moe_gain, routes,
    route_logits, w_gate, w_up, w_down,
):
    count = lax.axis_size("blk")
    me = lax.axis_index("blk").astype(jnp.int32)
    tok = hidden_in.shape[0]
    heads = w_key_up.shape[1] // NOPE
    experts = w_gate.shape[0] * count
    index = me[None]
    payload, latent, trig, reach = prepare(
        index, lengths, hidden_in, attn_gain, parents, routes, route_logits, w_query, w_latent,
        heads, experts,
    )
    queries = gather_blocks(payload, count)

    compressed = join_heads(latent)
    low = compressed[:, :RANK]
    low = low * lax.rsqrt(jnp.mean(low * low, axis=-1, keepdims=True) + EPSILON) * kv_gain
    first, second = compressed[:, RANK : RANK + HALF], compressed[:, RANK + HALF :]
    cosine, sine = trig[:, :HALF], trig[:, LANES : LANES + HALF]
    draft_rows = jnp.concatenate(
        [low, first * cosine - second * sine, second * cosine + first * sine], axis=-1
    ).astype(bf16)

    keys, values = expand(cache_rows, w_key_up, w_value_up, heads)
    slots = slot_request.shape[0]
    block = cache_rows.shape[0] // slots
    owner = jnp.maximum(slot_request, 0)
    owner_length = jnp.sum(
        jnp.where(owner[:, None] == jnp.arange(lengths.shape[0])[None, :], lengths[None, :], 0), axis=1
    )
    live = jnp.where(slot_request >= 0, owner_length - slot_block * block, 0)
    place = place_of(owner ^ me, count)
    partial, mixes = attend_slots(place, live, index, keys, values, queries, heads, block, experts)
    parts = scatter_blocks(partial, count)
    own = attend_own(draft_rows, payload, reach, w_key_up, w_value_up, heads)
    mine, other = sum_heads(project_out(w_out, own, parts, heads, tok))
    resid, moe_in = norm(hidden_in, mine, other, moe_gain)

    node = jnp.arange(tok, dtype=jnp.int32)
    pick = (accepted.reshape(-1)[:, None] == node[None, :]).astype(bf16)
    chosen = jnp.dot(pick, draft_rows, preferred_element_type=f32).astype(bf16)
    target = new_slots.reshape(-1, 1)
    tail = jnp.concatenate([target // 256, target % 256], axis=1).astype(bf16)
    packed = jnp.concatenate(
        [chosen, tail, jnp.zeros((chosen.shape[0], LANES - ROPE - 2), bf16)], axis=1
    )

    (radix, stride), *rest = phases(count)
    pieces = [moe_in] + [swap(moe_in, "blk", stride * j) for j in range(1, radix)]
    packed, pieces[-1] = lax.optimization_barrier((packed, pieces[-1]))
    tokens = [jnp.stack(pieces)]
    rows = [jnp.stack([packed] + [swap(packed, "blk", stride * j) for j in range(1, radix)])]
    for _, step in rest[:-1]:
        tokens = tokens + [swap(t, "blk", step) for t in tokens]
    half, near = len(tokens), rest[-1][1]
    kept, got = [], []
    for i in range(half):
        if i:
            tokens[i], kept[-1], sent, rows = lax.optimization_barrier(
                (tokens[i], kept[-1], sent, rows)
            )
        far = swap(tokens[i], "blk", near)
        keep, sent = expert(tokens[i], far, mixes[i], mixes[i + half], w_gate, w_up, w_down)
        if not i:
            rows[0], keep = lax.optimization_barrier((rows[0], keep))
            for _, step in rest:
                rows = rows + [swap(r, "blk", step) for r in rows]
        kept.append(keep)
        got.append(sent)
    sums = [add16(k, swap(g, "blk", near)) for k, g in zip(kept, got)]
    back = scatter_blocks(sums, count, near)

    rows = jnp.concatenate(rows)
    rows = rows.reshape(-1, packed.shape[1])
    at = RANK + ROPE
    slot = rows[:, at].astype(f32) * 256.0 + rows[:, at + 1].astype(f32)
    here = (me * NEW_DEV + jnp.arange(NEW_DEV, dtype=jnp.int32)).astype(f32)
    new_rows = jnp.dot(
        (here[:, None] == slot[None, :]).astype(bf16), rows[:, :at], preferred_element_type=f32
    ).astype(bf16)

    total = back[0].astype(f32)
    for value in back[1:]:
        total = total + value.astype(f32)
    mine, other = sum_heads(total.astype(bf16))
    routed = mine.astype(f32) + other.astype(f32)
    layer_out = (resid.astype(f32) + routed).astype(bf16)
    return (layer_out, new_rows)


def solution(mesh):
    return jax.shard_map(
        shards,
        mesh=mesh,
        in_specs=(
            P("blk", None),
            P(),
            P("head", None),
            P("head", None),
            P(),
            P(None, "head"),
            P(None, "head"),
            P("head", None),
            P("blk", None),
            P("blk"),
            P("blk"),
            P(),
            P("blk", None),
            P("blk", None),
            P("blk", None),
            P(),
            P("blk", None),
            P("blk", None),
            P("blk", "head", None),
            P("blk", "head", None),
            P("blk", "head", None),
        ),
        out_specs=(P("blk", None), P("blk", None)),
        check_vma=False,
    )
```

```python
import functools

import jax
import jax.numpy as jnp
from jax import lax
from jax.experimental import pallas as pl
from jax.experimental.pallas import tpu as pltpu
from jax.sharding import PartitionSpec as P

NOPE = 128
ROPE = 64
HALF = ROPE // 2
VDIM = 128
RANK = 512
NEW_DEV = 16
LANES = 128

EPSILON = 1e-06
ROUTE_SCALE = 2.446
ROPE_BASE = 50000.0
MIB = 1 << 20

f32 = jnp.float32
bf16 = jnp.bfloat16


def params(mib):
    return pltpu.CompilerParams(vmem_limit_bytes=mib * MIB)


def cost(flops, nbytes, trans=0):
    return pl.CostEstimate(flops=flops, bytes_accessed=nbytes, transcendentals=trans)


def nt(left, right):
    return lax.dot_general(left, right, (((1,), (1,)), ((), ())), preferred_element_type=f32)


def nn(left, right):
    return jnp.dot(left, right, preferred_element_type=f32)


def phases(count):
    out, stride = [], count
    while stride > 1:
        radix = 4 if stride == count and count >= 4 else 2
        stride //= radix
        out.append((radix, stride))
    return out


def swap(value, axis, bit):
    count = lax.axis_size(axis)
    return lax.ppermute(value, axis, [(i, i ^ bit) for i in range(count)])


def gather_blocks(value, count):
    (radix, stride), *rest = phases(count)
    pieces = [jnp.stack([value] + [swap(value, "blk", stride * j) for j in range(1, radix)])]
    for _, stride in rest:
        pieces = pieces + [swap(p, "blk", stride) for p in pieces]
    return pieces


def after(value, *others):
    return lax.optimization_barrier((value, *others))[0]


def add16(left, right):
    return (left.astype(f32) + right.astype(f32)).astype(bf16)


def fold_blocks(pieces, count):
    for _, stride in reversed(phases(count)[1:]):
        half = len(pieces) // 2
        got = [swap(p, "blk", stride) for p in pieces[half:]]
        pieces = [add16(p, g) for p, g in zip(pieces[:half], got)]
    return pieces[0]


def trade_blocks(value, count):
    radix, stride = phases(count)[0]
    return [value[0]] + [swap(value[j], "blk", stride * j) for j in range(1, radix)]


def place_of(relative, count):
    (radix, stride), *rest = phases(count)
    place = relative // stride
    size = radix
    for _, step in rest:
        place = place + (relative // step) % 2 * size
        size *= 2
    return place


def pre_kernel(
    heads, experts, place_ref, len_ref, hidden_ref, gain_ref, parents_ref, routes_ref, logits_ref,
    query_hbm, latent_hbm, out_ref, latent_ref, trig_ref, reach_ref, wq, wl, sems,
):
    copy_q = pltpu.make_async_copy(query_hbm, wq, sems.at[0])
    copy_l = pltpu.make_async_copy(latent_hbm, wl, sems.at[1])
    copy_q.start()
    copy_l.start()
    tok = hidden_ref.shape[0]
    rows = lax.broadcasted_iota(jnp.int32, (tok, tok), 0)
    cols = lax.broadcasted_iota(jnp.int32, (tok, tok), 1)
    eye = (rows == cols).astype(f32)
    below = jnp.where(rows == parents_ref[...], 1.0, 0.0) + eye
    for _ in range(max(1, (tok - 1).bit_length())):
        step = below.astype(bf16)
        below = jnp.minimum(nn(step, step), 1.0)
    reach = nt(eye.astype(bf16), below.astype(bf16))
    reach_ref[...] = reach
    depth = jnp.sum(reach, axis=-1, keepdims=True) - 1.0
    position = len_ref[place_ref[0]].astype(f32) + depth
    lane = lax.broadcasted_iota(jnp.int32, (1, LANES), 1)
    freqs = ROPE_BASE ** (-2.0 * (lane % HALF).astype(f32) / ROPE)
    angles = position * freqs
    cosine, sine = jnp.cos(angles), jnp.sin(angles)
    trig_ref[:, :LANES] = cosine
    trig_ref[:, LANES:] = sine
    sigma = jax.nn.sigmoid(logits_ref[...])
    weight = ROUTE_SCALE * sigma / jnp.sum(sigma, axis=0, keepdims=True)
    named = lax.broadcasted_iota(jnp.int32, (LANES, 1), 0)
    mix = jnp.zeros((LANES, tok), f32)
    for k in range(weight.shape[0]):
        mix = mix + jnp.where(named % experts == routes_ref[k : k + 1], weight[k : k + 1], 0.0)
    high = mix.astype(bf16).astype(f32)
    mix = jnp.where(named < experts, high, jnp.where(named < 2 * experts, mix - high, 0.0))
    mix = nt(eye.astype(bf16), mix.astype(bf16))
    hidden = hidden_ref[...].astype(f32)
    mean_square = jnp.mean(hidden * hidden, axis=-1, keepdims=True)
    normed = (hidden * lax.rsqrt(mean_square + EPSILON) * gain_ref[...]).astype(bf16)
    copy_q.wait()
    size = NOPE + ROPE
    for h in range(heads):
        part = nt(normed, wq[h * size : h * size + NOPE])
        out_ref[:, h * NOPE : (h + 1) * NOPE] = part.astype(bf16)
    pad = [jnp.zeros((LANES - heads * HALF, wq.shape[1]), bf16)] if heads * HALF < LANES else []
    first, second = (
        nt(normed, jnp.concatenate(
            [wq[h * size + NOPE + at : h * size + NOPE + at + HALF] for h in range(heads)] + pad))
        for at in (0, HALF)
    )
    base = heads * NOPE
    out_ref[:, base : base + LANES] = (first * cosine - second * sine).astype(bf16)
    out_ref[:, base + LANES : base + 2 * LANES] = (second * cosine + first * sine).astype(bf16)
    out_ref[:, base + 2 * LANES :] = mix.astype(bf16)
    copy_l.wait()
    latent_ref[...] = nt(normed, wl[...])


def prepare(place, lengths, hidden, gain, parents, routes, logits, w_query, w_latent, heads, experts):
    tok, width = hidden.shape
    smem = pl.BlockSpec(memory_space=pltpu.SMEM)
    hbm = pl.BlockSpec(memory_space=pltpu.HBM)
    lanes = heads * NOPE + 3 * LANES
    small = (hidden, gain[None], parents, routes.T, logits.T)
    whole = lambda shape: pl.BlockSpec(shape, lambda i: (0,) * len(shape))
    return pl.pallas_call(
        functools.partial(pre_kernel, heads, experts),
        grid=(1,),
        out_shape=(
            jax.ShapeDtypeStruct((tok, lanes), bf16),
            jax.ShapeDtypeStruct((tok, w_latent.shape[0]), f32),
            jax.ShapeDtypeStruct((tok, 2 * LANES), f32),
            jax.ShapeDtypeStruct((tok, tok), f32),
        ),
        in_specs=[smem, smem, *(whole(v.shape) for v in small), hbm, hbm],
        out_specs=tuple(
            whole(shape)
            for shape in ((tok, lanes), (tok, w_latent.shape[0]), (tok, 2 * LANES), (tok, tok))
        ),
        scratch_shapes=[
            pltpu.VMEM(w_query.shape, bf16),
            pltpu.VMEM(w_latent.shape, bf16),
            pltpu.SemaphoreType.DMA((2,)),
        ],
        compiler_params=params(56),
        cost_estimate=cost(2 * tok * width * 1100, 2 * width * 1100),
        name="prepare",
    )(place, lengths, *small, w_query, w_latent)


def spread(heads):
    row = lax.broadcasted_iota(jnp.int32, (ROPE, 2 * LANES), 0)
    col = lax.broadcasted_iota(jnp.int32, (ROPE, 2 * LANES), 1)
    inside = col % LANES < heads * HALF
    return jnp.where((row == col // LANES * HALF + col % HALF) & inside, 1.0, 0.0).astype(bf16)


def keys_values(rows, key_up, value_up, heads):
    low = rows[:, :RANK]
    nope = nn(low, key_up).astype(bf16)
    rope = nn(rows[:, RANK:], spread(heads)).astype(bf16)
    return jnp.concatenate([nope, rope], axis=-1), nn(low, value_up).astype(bf16)


def expand_kernel(heads, rows_ref, key_ref, value_ref, keys_out, values_out):
    keys_out[...], values_out[...] = keys_values(rows_ref[...], key_ref[...], value_ref[...], heads)


def expand(rows, key_up, value_up, heads):
    vmem = pl.BlockSpec(memory_space=pltpu.VMEM)
    count = rows.shape[0]
    return pl.pallas_call(
        functools.partial(expand_kernel, heads),
        out_shape=(
            jax.ShapeDtypeStruct((count, heads * NOPE + 2 * LANES), bf16),
            jax.ShapeDtypeStruct((count, heads * VDIM), bf16),
        ),
        in_specs=[vmem] * 3,
        out_specs=(vmem,) * 2,
        compiler_params=params(16),
        cost_estimate=cost(4 * count * RANK * heads * NOPE, 4 * count * RANK),
        name="expand",
    )(rows, key_up, value_up)


def by_head(query, heads):
    tok, lanes = query.shape[0], heads * NOPE + 2 * LANES
    lane = lax.broadcasted_iota(jnp.int32, (1, lanes), 1)
    head = jnp.where(lane < heads * NOPE, lane // NOPE, lane % LANES // HALF)
    query = query[:, :lanes].astype(f32)
    return jnp.concatenate(
        [jnp.where(head == h, query, 0.0) for h in range(heads)], axis=0
    ).astype(bf16)


def attend(query, keys, values, seen, heads):
    tok = query.shape[0] // heads
    scale = (NOPE + ROPE) ** (-0.5)
    weight = jnp.where(seen, jnp.exp(nt(query, keys) * scale), 0.0)
    high = weight.astype(bf16)
    low = (weight - high.astype(f32)).astype(bf16)
    full = nn(high, values)
    numer = jnp.concatenate(
        [full[h * tok : (h + 1) * tok, h * VDIM : (h + 1) * VDIM] for h in range(heads)], axis=0
    )
    ones = jnp.ones((16, keys.shape[0]), bf16)
    denom = nt(ones, high) + nt(ones, low)
    if denom.shape[1] < LANES:
        denom = jnp.concatenate([denom, jnp.zeros((16, LANES - denom.shape[1]), f32)], axis=-1)
    return jnp.concatenate([numer, denom], axis=0)


def slots_kernel(
    heads, slots, block, pieces, experts, place_ref, live_ref, index_ref, keys_ref, values_ref, *refs
):
    queries, outs, mix = refs[:pieces], refs[pieces : 2 * pieces], refs[2 * pieces]
    each, tok, lanes = queries[0].shape
    named = lax.broadcasted_iota(jnp.int32, (1, LANES), 1)
    mine = (named == index_ref[0]) | (named == index_ref[0] + experts)
    for i, query in enumerate(queries):
        shares = query[:, :, lanes - LANES :].reshape(each * tok, LANES).astype(f32)
        share = jnp.sum(jnp.where(mine, shares, 0.0), axis=-1, keepdims=True)
        mix[i * each : (i + 1) * each] = share.reshape(each, tok, 1)
    for out in outs:
        out[...] = jnp.zeros(out.shape, out.dtype)
    parts = []
    lane = lax.broadcasted_iota(jnp.int32, (1, block), 1)
    for s in range(slots):
        place = place_ref[s]
        query = queries[0][place % each]
        for p in range(1, pieces):
            query = jnp.where(place // each == p, queries[p][place % each], query)
        keys, values = (r[s * block : (s + 1) * block] for r in (keys_ref, values_ref))
        parts.append(attend(by_head(query, heads), keys, values, lane < live_ref[s], heads))
    for s in range(slots):
        place = place_ref[s]
        total = parts[s]
        for other in range(slots):
            if other != s:
                total = total + jnp.where(place_ref[other] == place, parts[other], 0.0)
        for p, out in enumerate(outs):
            @pl.when(place // each == p)
            def _():
                out[place % each] = total.astype(bf16)


def attend_slots(place, live, index, keys, values, queries, heads, block, experts):
    smem = pl.BlockSpec(memory_space=pltpu.SMEM)
    vmem = pl.BlockSpec(memory_space=pltpu.VMEM)
    slots, each, tok = place.shape[0], queries[0].shape[0], queries[0].shape[1]
    pieces = len(queries)
    out = jax.ShapeDtypeStruct((each, heads * tok + 16, LANES), bf16)
    mix = jax.ShapeDtypeStruct((pieces * each, tok, 1), f32)
    results = pl.pallas_call(
        functools.partial(slots_kernel, heads, slots, block, pieces, experts),
        out_shape=(out,) * pieces + (mix,),
        in_specs=[smem, smem, smem, vmem, vmem] + [vmem] * pieces,
        out_specs=(vmem,) * (pieces + 1),
        compiler_params=params(24),
        cost_estimate=cost(1 << 28, 2 << 20),
        name="attend_slots",
    )(place, live, index, keys, values, *queries)
    return list(results[:pieces]), results[pieces]


def own_kernel(heads, rows_ref, query_ref, reach_ref, key_ref, value_ref, out_ref):
    keys, values = keys_values(rows_ref[...], key_ref[...], value_ref[...], heads)
    seen = jnp.concatenate([reach_ref[...]] * heads, axis=0) > 0.5
    out_ref[...] = attend(by_head(query_ref[...], heads), keys, values, seen, heads)


def attend_own(rows, query, reach, key_up, value_up, heads):
    vmem = pl.BlockSpec(memory_space=pltpu.VMEM)
    return pl.pallas_call(
        functools.partial(own_kernel, heads),
        out_shape=jax.ShapeDtypeStruct((heads * rows.shape[0] + 16, LANES), f32),
        in_specs=[vmem] * 5,
        out_specs=vmem,
        compiler_params=params(16),
        cost_estimate=cost(1 << 26, 2 << 20),
        name="attend_own",
    )(rows, query, reach, key_up, value_up)


def project_kernel(heads, parts, w_ref, own_ref, *refs):
    total = own_ref[...]
    for ref in refs[:parts]:
        total = total + ref[...].astype(f32)
    count = heads * (total.shape[0] - 16) // heads
    tok = count // heads
    row = lax.broadcasted_iota(jnp.int32, (count, LANES), 0)
    col = lax.broadcasted_iota(jnp.int32, (count, LANES), 1)
    denom = jnp.sum(jnp.where(row == col, total[count : count + 1], 0.0), axis=-1, keepdims=True)
    attended = (total[:count] / denom).astype(bf16)
    wide = jnp.concatenate([attended[h * tok : (h + 1) * tok] for h in range(heads)], axis=-1)
    refs[parts][...] = nn(wide, w_ref[...]).astype(bf16)


def project_out(w_out, own, parts, heads, tok):
    vmem = pl.BlockSpec(memory_space=pltpu.VMEM)
    return pl.pallas_call(
        functools.partial(project_kernel, heads, len(parts)),
        out_shape=jax.ShapeDtypeStruct((tok, w_out.shape[1]), bf16),
        in_specs=[vmem] * (2 + len(parts)),
        out_specs=vmem,
        compiler_params=params(16),
        cost_estimate=cost(2 * tok * w_out.size, 2 * w_out.size),
        name="project_out",
    )(w_out, own, *parts)


def norm_kernel(hidden_ref, mine_ref, other_ref, gain_ref, packed_ref, resid_ref, out_ref):
    added = mine_ref[...].astype(f32) + other_ref[...].astype(f32)
    resid = (hidden_ref[...].astype(f32) + added).astype(bf16)
    resid_ref[...] = resid
    value = resid.astype(f32)
    mean_square = jnp.mean(value * value, axis=-1, keepdims=True)
    width = value.shape[1]
    out_ref[:, :width] = (value * lax.rsqrt(mean_square + EPSILON) * gain_ref[...]).astype(bf16)
    out_ref[:, width:] = packed_ref[...]


def norm(hidden, mine, other, gain, packed):
    tok, width = hidden.shape
    vmem = pl.BlockSpec(memory_space=pltpu.VMEM)
    return pl.pallas_call(
        norm_kernel,
        out_shape=(
            jax.ShapeDtypeStruct((tok, width), bf16),
            jax.ShapeDtypeStruct((tok, width + packed.shape[1]), bf16),
        ),
        in_specs=[vmem] * 5,
        out_specs=(vmem, vmem),
        compiler_params=params(8),
        name="norm",
    )(hidden, mine, other, gain[None], packed)


def expert_kernel(parts, cuts, *refs):
    blocks = sum(cuts)
    tokens, mixes, outs = refs[:parts], refs[parts : parts + blocks], refs[parts + blocks + 3 :]
    gate, up, down = refs[parts + blocks : parts + blocks + 3]
    tok, width = tokens[0].shape[1:]
    rows = jnp.concatenate([r[i] for r in tokens for i in range(r.shape[0])], axis=0)
    weight = jnp.concatenate([m[0] for m in mixes], axis=0)
    gated = nt(rows, gate[0])
    gated = gated / (1.0 + jnp.exp(-gated))
    act = (gated * nt(rows, up[0])).astype(bf16)
    out = (nn(act, down[0]) * weight).astype(bf16)
    at = 0
    for ref, size in zip(outs, cuts):
        ref[...] = out[at * tok : (at + size) * tok].reshape(size, tok, width)
        at += size


def expert(tokens, places, mix, weights, cuts):
    vmem = pl.BlockSpec(memory_space=pltpu.VMEM)
    parts, size = len(tokens), weights[0].size
    tok, width = tokens[0].shape[1], weights[0].shape[2]
    blocks = [pl.BlockSpec((t.shape[0], tok, width), lambda i: (0, 0, 0)) for t in tokens]
    shares = [pl.BlockSpec((1, tok, 1), lambda i, at=at: (at, 0, 0)) for at in places]
    return pl.pallas_call(
        functools.partial(expert_kernel, parts, cuts),
        grid=(1,),
        out_shape=tuple(jax.ShapeDtypeStruct((cut, tok, width), bf16) for cut in cuts),
        in_specs=blocks + shares + [vmem] * len(weights),
        out_specs=tuple(pl.BlockSpec((cut, tok, width), lambda i: (0, 0, 0)) for cut in cuts),
        compiler_params=params(20),
        cost_estimate=cost(6 * tok * len(places) * size, 6 * size),
        name="expert",
    )(*tokens, *(mix for _ in places), *weights)


def pack_rows(rows, tok):
    count, width = rows.shape
    lanes = -(-width // (tok // count * LANES)) * LANES
    rows = jnp.pad(rows, ((0, 0), (0, tok // count * lanes - width)))
    return jnp.concatenate([rows[:, at : at + lanes] for at in range(0, rows.shape[1], lanes)])


def rows_kernel(count, index_ref, *refs):
    out_ref = refs[-1]
    target = index_ref[0] * NEW_DEV + lax.broadcasted_iota(jnp.int32, (1, NEW_DEV), 1)
    width = out_ref.shape[1]
    rows = []
    for wide in [ref[i].astype(f32) for ref in refs[:-1] for i in range(ref.shape[0])]:
        parts = [wide[at : at + count] for at in range(0, wide.shape[0], count)]
        rows.append(jnp.concatenate(parts, axis=-1))
    rows = jnp.concatenate(rows, axis=0)
    slot = (rows[:, width : width + 1] * 256.0 + rows[:, width + 1 : width + 2]).astype(jnp.int32)
    here = jnp.where(slot == target, 1.0, 0.0).astype(bf16)
    out_ref[...] = lax.dot_general(
        here, rows[:, :width].astype(bf16), (((0,), (0,)), ((), ())), preferred_element_type=f32
    ).astype(bf16)


def place_rows(index, pieces, count, width):
    smem = pl.BlockSpec(memory_space=pltpu.SMEM)
    out = (NEW_DEV, RANK + ROPE)
    lanes = pieces[0].shape[2] - width
    blocks = [pl.BlockSpec((*p.shape[:2], lanes), lambda i: (0, 0, width // lanes)) for p in pieces]
    return pl.pallas_call(
        functools.partial(rows_kernel, count),
        grid=(1,),
        out_shape=jax.ShapeDtypeStruct(out, bf16),
        in_specs=[smem] + blocks,
        out_specs=pl.BlockSpec(out, lambda i: (0, 0)),
        compiler_params=params(8),
        name="place_rows",
    )(index, *pieces)


def sum_heads(value):
    count, bit = lax.axis_size("head"), 1
    other = swap(value, "head", bit)
    while 2 * bit < count:
        bit *= 2
        value = add16(value, other)
        other = swap(value, "head", bit)
    return value, other


def join_heads(value):
    if lax.axis_size("head") == 2:
        other = swap(value, "head", 1)
        first = lax.axis_index("head") == 0
        parts = [jnp.where(first, value, other), jnp.where(first, other, value)]
        return jnp.concatenate(parts, axis=1)
    return lax.all_gather(value, "head", axis=1, tiled=True)


def shards(
    hidden_in, attn_gain, w_query, w_latent, kv_gain, w_key_up, w_value_up, w_out, cache_rows,
    slot_request, slot_block, lengths, parents, accepted, new_slots, moe_gain, routes,
    route_logits, w_gate, w_up, w_down,
):
    count = lax.axis_size("blk")
    me = lax.axis_index("blk").astype(jnp.int32)
    tok = hidden_in.shape[0]
    heads = w_key_up.shape[1] // NOPE
    experts = w_gate.shape[0] * count
    index = me[None]
    payload, latent, trig, reach = prepare(
        index, lengths, hidden_in, attn_gain, parents, routes, route_logits, w_query, w_latent,
        heads, experts,
    )
    queries = gather_blocks(payload, count)

    compressed = join_heads(latent)
    low = compressed[:, :RANK]
    low = low * lax.rsqrt(jnp.mean(low * low, axis=-1, keepdims=True) + EPSILON) * kv_gain
    first, second = compressed[:, RANK : RANK + HALF], compressed[:, RANK + HALF :]
    cosine, sine = trig[:, :HALF], trig[:, LANES : LANES + HALF]
    draft_rows = jnp.concatenate(
        [low, first * cosine - second * sine, second * cosine + first * sine], axis=-1
    ).astype(bf16)

    keys, values = expand(cache_rows, w_key_up, w_value_up, heads)
    slots = slot_request.shape[0]
    block = cache_rows.shape[0] // slots
    owner = jnp.maximum(slot_request, 0)
    owner_length = jnp.sum(
        jnp.where(owner[:, None] == jnp.arange(lengths.shape[0])[None, :], lengths[None, :], 0), axis=1
    )
    live = jnp.where(slot_request >= 0, owner_length - slot_block * block, 0)
    place = place_of(owner ^ me, count)
    partial, mix = attend_slots(place, live, index, keys, values, queries, heads, block, experts)
    node = jnp.arange(tok, dtype=jnp.int32)
    pick = (accepted.reshape(-1)[:, None] == node[None, :]).astype(bf16)
    chosen = jnp.dot(pick, draft_rows, preferred_element_type=f32).astype(bf16)
    target = new_slots.reshape(-1, 1)
    tail = jnp.concatenate([target // 256, target % 256], axis=1).astype(bf16)
    packed = pack_rows(jnp.concatenate([chosen, tail], axis=1), tok)

    own = attend_own(draft_rows, payload, reach, w_key_up, w_value_up, heads)
    parts = trade_blocks(fold_blocks(partial, count), count)
    mine, other = sum_heads(project_out(w_out, own, parts, heads, tok))
    resid, moe_in = norm(hidden_in, mine, other, moe_gain, packed)

    (radix, stride), *rest = phases(count)
    near, half, mid = rest[-1][1], 1 << (len(rest) - 1), radix // 2
    weights = (w_gate, w_up, w_down)
    first = [swap(moe_in, "blk", stride * j) for j in range(1, radix)]
    mine = [moe_in[None]]
    for _, step in rest[:-1]:
        mine = mine + [swap(t, "blk", step) for t in mine]
    first[-1] = after(first[-1], *mine[1:])
    others = [jnp.stack(first)]
    for _, step in rest[:-1]:
        others = others + [swap(t, "blk", step) for t in others]
    tokens = [list(pair) for pair in zip(mine, others)]
    kept, sent = [], []
    cuts = [mid] + [1] * (radix - mid)
    for i in range(half):
        pair = tokens[i]
        if i:
            pair[1] = after(pair[1], kept[-1][0], sent[-1][0])
        far = [swap(t, "blk", near) for t in pair]
        tokens.append(far)
        places = [at * radix + j for at in (i, i + half) for j in range(radix)]
        inner = cuts if i + 1 == half else [radix]
        done = list(expert(pair + far, places, mix, weights, cuts + inner))
        kept.append(done[: len(cuts)])
        sent.append(done[len(cuts) :])
    order = [*range(1, len(cuts)), 0]
    sums = []
    for i in range(half):
        if i + 1 == half:
            got = [None] * len(cuts)
            for at in order:
                got[at] = swap(sent[i][at], "blk", near)
        else:
            got = swap(sent[i][0], "blk", near)
            got = [got[:mid]] + [got[j : j + 1] for j in range(mid, radix)]
        sums.append([add16(k, g) for k, g in zip(kept[i], got)])
    for _, step in reversed(rest[:-1]):
        part = len(sums) // 2
        for i in range(part):
            last = None
            for at in order:
                value = sums[part + i][at]
                value = value if last is None else after(value, last)
                last = sums[part + i][at] = value
        got = [[swap(v, "blk", step) for v in values] for values in sums[part:]]
        for i in range(part):
            last = None
            for at in order:
                value = got[i][at] if last is None else after(got[i][at], last)
                last = sums[i][at] = add16(sums[i][at], value)
        sums = sums[:part]
    (sums,) = sums
    back = [swap(sums[at][0], "blk", stride * (mid + at - 1)) for at in order[:-1]]
    back += [swap(sums[0][j], "blk", stride * j) for j in range(1, mid)]
    total = sums[0][0].astype(f32)
    for value in reversed(back):
        total = total + value.astype(f32)
    mine, other = sum_heads(total.astype(bf16))
    layer_out = (resid.astype(f32) + (mine.astype(f32) + other.astype(f32))).astype(bf16)
    pieces = [piece for group in tokens for piece in group]
    new_rows = place_rows(index, pieces, accepted.shape[1], hidden_in.shape[1])
    return (layer_out, new_rows)


def solution(mesh):
    return jax.shard_map(
        shards,
        mesh=mesh,
        in_specs=(
            P("blk", None),
            P(),
            P("head", None),
            P("head", None),
            P(),
            P(None, "head"),
            P(None, "head"),
            P("head", None),
            P("blk", None),
            P("blk"),
            P("blk"),
            P(),
            P("blk", None),
            P("blk", None),
            P("blk", None),
            P(),
            P("blk", None),
            P("blk", None),
            P("blk", "head", None),
            P("blk", "head", None),
            P("blk", "head", None),
        ),
        out_specs=(P("blk", None), P("blk", None)),
        check_vma=False,
    )
```

```python
import functools

import jax
import jax.numpy as jnp
from jax import lax
from jax.experimental import pallas as pl
from jax.experimental.pallas import tpu as pltpu
from jax.sharding import PartitionSpec as P

NOPE = 128
ROPE = 64
HALF = ROPE // 2
VDIM = 128
RANK = 512
NEW_DEV = 16
LANES = 128

EPSILON = 1e-06
ROUTE_SCALE = 2.446
ROPE_BASE = 50000.0
MIB = 1 << 20

f32 = jnp.float32
bf16 = jnp.bfloat16


def params(mib):
    return pltpu.CompilerParams(vmem_limit_bytes=mib * MIB)


def cost(flops, nbytes, trans=0):
    return pl.CostEstimate(flops=flops, bytes_accessed=nbytes, transcendentals=trans)


def nt(left, right):
    return lax.dot_general(left, right, (((1,), (1,)), ((), ())), preferred_element_type=f32)


def nn(left, right):
    return jnp.dot(left, right, preferred_element_type=f32)


def phases(count):
    out, stride = [], count
    while stride > 1:
        radix = 4 if stride == count and count >= 4 else 2
        stride //= radix
        out.append((radix, stride))
    return out


def swap(value, axis, bit):
    count = lax.axis_size(axis)
    return lax.ppermute(value, axis, [(i, i ^ bit) for i in range(count)])


def gather_blocks(value, count):
    (radix, stride), *rest = phases(count)
    pieces = [jnp.stack([value] + [swap(value, "blk", stride * j) for j in range(1, radix)])]
    for _, stride in rest:
        pieces = pieces + [swap(p, "blk", stride) for p in pieces]
    return pieces


def after(value, *others):
    return lax.optimization_barrier((value, *others))[0]


def add16(left, right):
    return (left.astype(f32) + right.astype(f32)).astype(bf16)


def fold_blocks(pieces, count):
    for _, stride in reversed(phases(count)[1:]):
        half = len(pieces) // 2
        got = [swap(p, "blk", stride) for p in pieces[half:]]
        pieces = [add16(p, g) for p, g in zip(pieces[:half], got)]
    return pieces[0]


def trade_blocks(value, count):
    radix, stride = phases(count)[0]
    return [value[0]] + [swap(value[j], "blk", stride * j) for j in range(1, radix)]


def place_of(relative, count):
    (radix, stride), *rest = phases(count)
    place = relative // stride
    size = radix
    for _, step in rest:
        place = place + (relative // step) % 2 * size
        size *= 2
    return place


def pre_kernel(
    heads, experts, query_hbm, parents_hbm, lengths_hbm, routes_hbm, logits_hbm, hidden_hbm, gain_hbm,
    latent_hbm, out_ref, latent_ref, trig_ref, reach_ref, wq, parents_ref, len_ref, routes_ref,
    logits_ref, hidden_ref, gain_ref, wl, sems,
):
    copies = [
        pltpu.make_async_copy(src, dst, sems.at[i])
        for i, (src, dst) in enumerate((
            (query_hbm, wq), (parents_hbm, parents_ref), (lengths_hbm, len_ref),
            (routes_hbm, routes_ref), (logits_hbm, logits_ref), (hidden_hbm, hidden_ref),
            (gain_hbm, gain_ref), (latent_hbm, wl),
        ))
    ]
    for copy in copies[1:7] + copies[:1] + copies[7:]:
        copy.start()
    for copy in copies[1:7]:
        copy.wait()
    tok = hidden_ref.shape[0]
    rows = lax.broadcasted_iota(jnp.int32, (tok, tok), 0)
    cols = lax.broadcasted_iota(jnp.int32, (tok, tok), 1)
    eye = (rows == cols).astype(f32)
    below = jnp.where(rows == parents_ref[...], 1.0, 0.0) + eye
    for _ in range(max(1, (tok - 1).bit_length())):
        step = below.astype(bf16)
        below = jnp.minimum(nn(step, step), 1.0)
    reach = nt(eye.astype(bf16), below.astype(bf16))
    reach_ref[...] = reach
    depth = jnp.sum(reach, axis=-1, keepdims=True) - 1.0
    at = lax.broadcasted_iota(jnp.int32, len_ref.shape, 1) == lax.axis_index("blk")
    length = jnp.sum(jnp.where(at, len_ref[...].astype(f32), 0.0), axis=-1, keepdims=True)
    position = length + depth
    lane = lax.broadcasted_iota(jnp.int32, (1, LANES), 1)
    freqs = ROPE_BASE ** (-2.0 * (lane % HALF).astype(f32) / ROPE)
    angles = position * freqs
    cosine, sine = jnp.cos(angles), jnp.sin(angles)
    trig_ref[:, :LANES] = cosine
    trig_ref[:, LANES:] = sine
    sigma = jax.nn.sigmoid(logits_ref[...])
    weight = ROUTE_SCALE * sigma / jnp.sum(sigma, axis=0, keepdims=True)
    named = lax.broadcasted_iota(jnp.int32, (LANES, 1), 0)
    mix = jnp.zeros((LANES, tok), f32)
    for k in range(weight.shape[0]):
        mix = mix + jnp.where(named % experts == routes_ref[k : k + 1], weight[k : k + 1], 0.0)
    high = mix.astype(bf16).astype(f32)
    mix = jnp.where(named < experts, high, jnp.where(named < 2 * experts, mix - high, 0.0))
    mix = nt(eye.astype(bf16), mix.astype(bf16))
    hidden = hidden_ref[...].astype(f32)
    mean_square = jnp.mean(hidden * hidden, axis=-1, keepdims=True)
    normed = (hidden * lax.rsqrt(mean_square + EPSILON) * gain_ref[...]).astype(bf16)
    copies[0].wait()
    size = NOPE + ROPE
    for h in range(heads):
        part = nt(normed, wq[h * size : h * size + NOPE])
        out_ref[:, h * NOPE : (h + 1) * NOPE] = part.astype(bf16)
    pad = [jnp.zeros((LANES - heads * HALF, wq.shape[1]), bf16)] if heads * HALF < LANES else []
    first, second = (
        nt(normed, jnp.concatenate(
            [wq[h * size + NOPE + at : h * size + NOPE + at + HALF] for h in range(heads)] + pad))
        for at in (0, HALF)
    )
    base = heads * NOPE
    out_ref[:, base : base + LANES] = (first * cosine - second * sine).astype(bf16)
    out_ref[:, base + LANES : base + 2 * LANES] = (second * cosine + first * sine).astype(bf16)
    out_ref[:, base + 2 * LANES :] = mix.astype(bf16)
    copies[7].wait()
    latent_ref[...] = nt(normed, wl[...])


def prepare(lengths, hidden, gain, parents, routes, logits, w_query, w_latent, heads, experts):
    tok, width = hidden.shape
    vmem = pl.BlockSpec(memory_space=pltpu.VMEM)
    hbm = pl.BlockSpec(memory_space=pltpu.HBM)
    lanes = heads * NOPE + 3 * LANES
    args = (w_query, parents, lengths[None], routes.T, logits.T, hidden, gain[None], w_latent)
    return pl.pallas_call(
        functools.partial(pre_kernel, heads, experts),
        out_shape=(
            jax.ShapeDtypeStruct((tok, lanes), bf16),
            jax.ShapeDtypeStruct((tok, w_latent.shape[0]), f32),
            jax.ShapeDtypeStruct((tok, 2 * LANES), f32),
            jax.ShapeDtypeStruct((tok, tok), f32),
        ),
        in_specs=[hbm] * len(args),
        out_specs=(vmem,) * 4,
        scratch_shapes=[pltpu.VMEM(a.shape, a.dtype) for a in args]
        + [pltpu.SemaphoreType.DMA((len(args),))],
        compiler_params=params(58),
        cost_estimate=cost(2 * tok * width * 1100, 2 * width * 1100),
        name="prepare",
    )(*args)


def spread(heads):
    row = lax.broadcasted_iota(jnp.int32, (ROPE, 2 * LANES), 0)
    col = lax.broadcasted_iota(jnp.int32, (ROPE, 2 * LANES), 1)
    inside = col % LANES < heads * HALF
    return jnp.where((row == col // LANES * HALF + col % HALF) & inside, 1.0, 0.0).astype(bf16)


def keys_values(rows, key_up, value_up, heads):
    low = rows[:, :RANK]
    nope = nn(low, key_up).astype(bf16)
    rope = nn(rows[:, RANK:], spread(heads)).astype(bf16)
    return jnp.concatenate([nope, rope], axis=-1), nn(low, value_up).astype(bf16)


def expand_kernel(heads, rows_ref, key_ref, value_ref, keys_out, values_out):
    keys_out[...], values_out[...] = keys_values(rows_ref[...], key_ref[...], value_ref[...], heads)


def expand(rows, key_up, value_up, heads):
    vmem = pl.BlockSpec(memory_space=pltpu.VMEM)
    count = rows.shape[0]
    return pl.pallas_call(
        functools.partial(expand_kernel, heads),
        out_shape=(
            jax.ShapeDtypeStruct((count, heads * NOPE + 2 * LANES), bf16),
            jax.ShapeDtypeStruct((count, heads * VDIM), bf16),
        ),
        in_specs=[vmem] * 3,
        out_specs=(vmem,) * 2,
        compiler_params=params(16),
        cost_estimate=cost(4 * count * RANK * heads * NOPE, 4 * count * RANK),
        name="expand",
    )(rows, key_up, value_up)


def by_head(query, heads):
    tok, lanes = query.shape[0], heads * NOPE + 2 * LANES
    lane = lax.broadcasted_iota(jnp.int32, (1, lanes), 1)
    head = jnp.where(lane < heads * NOPE, lane // NOPE, lane % LANES // HALF)
    query = query[:, :lanes].astype(f32)
    return jnp.concatenate(
        [jnp.where(head == h, query, 0.0) for h in range(heads)], axis=0
    ).astype(bf16)


def attend(query, keys, values, seen, heads):
    tok = query.shape[0] // heads
    scale = (NOPE + ROPE) ** (-0.5)
    weight = jnp.where(seen, jnp.exp(nt(query, keys) * scale), 0.0)
    high = weight.astype(bf16)
    low = (weight - high.astype(f32)).astype(bf16)
    full = nn(high, values)
    numer = jnp.concatenate(
        [full[h * tok : (h + 1) * tok, h * VDIM : (h + 1) * VDIM] for h in range(heads)], axis=0
    )
    ones = jnp.ones((16, keys.shape[0]), bf16)
    denom = nt(ones, high) + nt(ones, low)
    if denom.shape[1] < LANES:
        denom = jnp.concatenate([denom, jnp.zeros((16, LANES - denom.shape[1]), f32)], axis=-1)
    return jnp.concatenate([numer, denom], axis=0)


def slots_kernel(
    heads, slots, block, pieces, experts, place_ref, live_ref, index_ref, keys_ref, values_ref, *refs
):
    queries, outs, mix = refs[:pieces], refs[pieces : 2 * pieces], refs[2 * pieces]
    each, tok, lanes = queries[0].shape
    named = lax.broadcasted_iota(jnp.int32, (1, LANES), 1)
    mine = (named == index_ref[0]) | (named == index_ref[0] + experts)
    for i, query in enumerate(queries):
        shares = query[:, :, lanes - LANES :].reshape(each * tok, LANES).astype(f32)
        share = jnp.sum(jnp.where(mine, shares, 0.0), axis=-1, keepdims=True)
        mix[i * each : (i + 1) * each] = share.reshape(each, tok, 1)
    for out in outs:
        out[...] = jnp.zeros(out.shape, out.dtype)
    parts = []
    lane = lax.broadcasted_iota(jnp.int32, (1, block), 1)
    for s in range(slots):
        place = place_ref[s]
        query = queries[0][place % each]
        for p in range(1, pieces):
            query = jnp.where(place // each == p, queries[p][place % each], query)
        keys, values = (r[s * block : (s + 1) * block] for r in (keys_ref, values_ref))
        parts.append(attend(by_head(query, heads), keys, values, lane < live_ref[s], heads))
    for s in range(slots):
        place = place_ref[s]
        total = parts[s]
        for other in range(slots):
            if other != s:
                total = total + jnp.where(place_ref[other] == place, parts[other], 0.0)
        for p, out in enumerate(outs):
            @pl.when(place // each == p)
            def _():
                out[place % each] = total.astype(bf16)


def attend_slots(place, live, index, keys, values, queries, heads, block, experts):
    smem = pl.BlockSpec(memory_space=pltpu.SMEM)
    vmem = pl.BlockSpec(memory_space=pltpu.VMEM)
    slots, each, tok = place.shape[0], queries[0].shape[0], queries[0].shape[1]
    pieces = len(queries)
    out = jax.ShapeDtypeStruct((each, heads * tok + 16, LANES), bf16)
    mix = jax.ShapeDtypeStruct((pieces * each, tok, 1), f32)
    results = pl.pallas_call(
        functools.partial(slots_kernel, heads, slots, block, pieces, experts),
        out_shape=(out,) * pieces + (mix,),
        in_specs=[smem, smem, smem, vmem, vmem] + [vmem] * pieces,
        out_specs=(vmem,) * (pieces + 1),
        compiler_params=params(24),
        cost_estimate=cost(1 << 28, 2 << 20),
        name="attend_slots",
    )(place, live, index, keys, values, *queries)
    return list(results[:pieces]), results[pieces]


def own_kernel(heads, rows_ref, query_ref, reach_ref, key_ref, value_ref, out_ref):
    keys, values = keys_values(rows_ref[...], key_ref[...], value_ref[...], heads)
    seen = jnp.concatenate([reach_ref[...]] * heads, axis=0) > 0.5
    out_ref[...] = attend(by_head(query_ref[...], heads), keys, values, seen, heads)


def attend_own(rows, query, reach, key_up, value_up, heads):
    vmem = pl.BlockSpec(memory_space=pltpu.VMEM)
    return pl.pallas_call(
        functools.partial(own_kernel, heads),
        out_shape=jax.ShapeDtypeStruct((heads * rows.shape[0] + 16, LANES), f32),
        in_specs=[vmem] * 5,
        out_specs=vmem,
        compiler_params=params(16),
        cost_estimate=cost(1 << 26, 2 << 20),
        name="attend_own",
    )(rows, query, reach, key_up, value_up)


def project_kernel(heads, parts, w_ref, own_ref, *refs):
    total = own_ref[...]
    for ref in refs[:parts]:
        total = total + ref[...].astype(f32)
    count = heads * (total.shape[0] - 16) // heads
    tok = count // heads
    row = lax.broadcasted_iota(jnp.int32, (count, LANES), 0)
    col = lax.broadcasted_iota(jnp.int32, (count, LANES), 1)
    denom = jnp.sum(jnp.where(row == col, total[count : count + 1], 0.0), axis=-1, keepdims=True)
    attended = (total[:count] / denom).astype(bf16)
    wide = jnp.concatenate([attended[h * tok : (h + 1) * tok] for h in range(heads)], axis=-1)
    refs[parts][...] = nn(wide, w_ref[...]).astype(bf16)


def project_out(w_out, own, parts, heads, tok):
    vmem = pl.BlockSpec(memory_space=pltpu.VMEM)
    return pl.pallas_call(
        functools.partial(project_kernel, heads, len(parts)),
        out_shape=jax.ShapeDtypeStruct((tok, w_out.shape[1]), bf16),
        in_specs=[vmem] * (2 + len(parts)),
        out_specs=vmem,
        compiler_params=params(16),
        cost_estimate=cost(2 * tok * w_out.size, 2 * w_out.size),
        name="project_out",
    )(w_out, own, *parts)


def norm_kernel(hidden_ref, mine_ref, other_ref, gain_ref, packed_ref, resid_ref, out_ref):
    added = mine_ref[...].astype(f32) + other_ref[...].astype(f32)
    resid = (hidden_ref[...].astype(f32) + added).astype(bf16)
    resid_ref[...] = resid
    value = resid.astype(f32)
    mean_square = jnp.mean(value * value, axis=-1, keepdims=True)
    width = value.shape[1]
    out_ref[:, :width] = (value * lax.rsqrt(mean_square + EPSILON) * gain_ref[...]).astype(bf16)
    out_ref[:, width:] = packed_ref[...]


def norm(hidden, mine, other, gain, packed):
    tok, width = hidden.shape
    vmem = pl.BlockSpec(memory_space=pltpu.VMEM)
    return pl.pallas_call(
        norm_kernel,
        out_shape=(
            jax.ShapeDtypeStruct((tok, width), bf16),
            jax.ShapeDtypeStruct((tok, width + packed.shape[1]), bf16),
        ),
        in_specs=[vmem] * 5,
        out_specs=(vmem, vmem),
        compiler_params=params(8),
        name="norm",
    )(hidden, mine, other, gain[None], packed)


def expert_kernel(parts, cuts, *refs):
    blocks = sum(cuts)
    tokens, mixes, outs = refs[:parts], refs[parts : parts + blocks], refs[parts + blocks + 3 :]
    gate, up, down = refs[parts + blocks : parts + blocks + 3]
    tok, width = tokens[0].shape[1:]
    rows = jnp.concatenate([r[i] for r in tokens for i in range(r.shape[0])], axis=0)
    weight = jnp.concatenate([m[0] for m in mixes], axis=0)
    gated = nt(rows, gate[0])
    gated = gated / (1.0 + jnp.exp(-gated))
    act = (gated * nt(rows, up[0])).astype(bf16)
    out = (nn(act, down[0]) * weight).astype(bf16)
    at = 0
    for ref, size in zip(outs, cuts):
        ref[...] = out[at * tok : (at + size) * tok].reshape(size, tok, width)
        at += size


def expert(tokens, places, mix, weights, cuts):
    vmem = pl.BlockSpec(memory_space=pltpu.VMEM)
    parts, size = len(tokens), weights[0].size
    tok, width = tokens[0].shape[1], weights[0].shape[2]
    blocks = [pl.BlockSpec((t.shape[0], tok, width), lambda i: (0, 0, 0)) for t in tokens]
    shares = [pl.BlockSpec((1, tok, 1), lambda i, at=at: (at, 0, 0)) for at in places]
    return pl.pallas_call(
        functools.partial(expert_kernel, parts, cuts),
        grid=(1,),
        out_shape=tuple(jax.ShapeDtypeStruct((cut, tok, width), bf16) for cut in cuts),
        in_specs=blocks + shares + [vmem] * len(weights),
        out_specs=tuple(pl.BlockSpec((cut, tok, width), lambda i: (0, 0, 0)) for cut in cuts),
        compiler_params=params(20),
        cost_estimate=cost(6 * tok * len(places) * size, 6 * size),
        name="expert",
    )(*tokens, *(mix for _ in places), *weights)


def pack_rows(rows, tok):
    count, width = rows.shape
    lanes = -(-width // (tok // count * LANES)) * LANES
    rows = jnp.pad(rows, ((0, 0), (0, tok // count * lanes - width)))
    return jnp.concatenate([rows[:, at : at + lanes] for at in range(0, rows.shape[1], lanes)])


def rows_kernel(count, index_ref, *refs):
    out_ref = refs[-1]
    target = index_ref[0] * NEW_DEV + lax.broadcasted_iota(jnp.int32, (1, NEW_DEV), 1)
    width = out_ref.shape[1]
    rows = []
    for wide in [ref[i].astype(f32) for ref in refs[:-1] for i in range(ref.shape[0])]:
        parts = [wide[at : at + count] for at in range(0, wide.shape[0], count)]
        rows.append(jnp.concatenate(parts, axis=-1))
    rows = jnp.concatenate(rows, axis=0)
    slot = (rows[:, width : width + 1] * 256.0 + rows[:, width + 1 : width + 2]).astype(jnp.int32)
    here = jnp.where(slot == target, 1.0, 0.0).astype(bf16)
    out_ref[...] = lax.dot_general(
        here, rows[:, :width].astype(bf16), (((0,), (0,)), ((), ())), preferred_element_type=f32
    ).astype(bf16)


def place_rows(index, pieces, count, width):
    smem = pl.BlockSpec(memory_space=pltpu.SMEM)
    out = (NEW_DEV, RANK + ROPE)
    lanes = pieces[0].shape[2] - width
    blocks = [pl.BlockSpec((*p.shape[:2], lanes), lambda i: (0, 0, width // lanes)) for p in pieces]
    return pl.pallas_call(
        functools.partial(rows_kernel, count),
        grid=(1,),
        out_shape=jax.ShapeDtypeStruct(out, bf16),
        in_specs=[smem] + blocks,
        out_specs=pl.BlockSpec(out, lambda i: (0, 0)),
        compiler_params=params(8),
        name="place_rows",
    )(index, *pieces)


def sum_heads(value):
    count, bit = lax.axis_size("head"), 1
    other = swap(value, "head", bit)
    while 2 * bit < count:
        bit *= 2
        value = add16(value, other)
        other = swap(value, "head", bit)
    return value, other


def join_heads(value):
    if lax.axis_size("head") == 2:
        other = swap(value, "head", 1)
        first = lax.axis_index("head") == 0
        parts = [jnp.where(first, value, other), jnp.where(first, other, value)]
        return jnp.concatenate(parts, axis=1)
    return lax.all_gather(value, "head", axis=1, tiled=True)


def shards(
    hidden_in, attn_gain, w_query, w_latent, kv_gain, w_key_up, w_value_up, w_out, cache_rows,
    slot_request, slot_block, lengths, parents, accepted, new_slots, moe_gain, routes,
    route_logits, w_gate, w_up, w_down,
):
    count = lax.axis_size("blk")
    me = lax.axis_index("blk").astype(jnp.int32)
    tok = hidden_in.shape[0]
    heads = w_key_up.shape[1] // NOPE
    experts = w_gate.shape[0] * count
    index = me[None]
    payload, latent, trig, reach = prepare(
        lengths, hidden_in, attn_gain, parents, routes, route_logits, w_query, w_latent,
        heads, experts,
    )
    queries = gather_blocks(payload, count)

    compressed = join_heads(latent)
    low = compressed[:, :RANK]
    low = low * lax.rsqrt(jnp.mean(low * low, axis=-1, keepdims=True) + EPSILON) * kv_gain
    first, second = compressed[:, RANK : RANK + HALF], compressed[:, RANK + HALF :]
    cosine, sine = trig[:, :HALF], trig[:, LANES : LANES + HALF]
    draft_rows = jnp.concatenate(
        [low, first * cosine - second * sine, second * cosine + first * sine], axis=-1
    ).astype(bf16)

    keys, values = expand(cache_rows, w_key_up, w_value_up, heads)
    slots = slot_request.shape[0]
    block = cache_rows.shape[0] // slots
    owner = jnp.maximum(slot_request, 0)
    owner_length = jnp.sum(
        jnp.where(owner[:, None] == jnp.arange(lengths.shape[0])[None, :], lengths[None, :], 0), axis=1
    )
    live = jnp.where(slot_request >= 0, owner_length - slot_block * block, 0)
    place = place_of(owner ^ me, count)
    partial, mix = attend_slots(place, live, index, keys, values, queries, heads, block, experts)
    node = jnp.arange(tok, dtype=jnp.int32)
    pick = (accepted.reshape(-1)[:, None] == node[None, :]).astype(bf16)
    chosen = jnp.dot(pick, draft_rows, preferred_element_type=f32).astype(bf16)
    target = new_slots.reshape(-1, 1)
    tail = jnp.concatenate([target // 256, target % 256], axis=1).astype(bf16)
    packed = pack_rows(jnp.concatenate([chosen, tail], axis=1), tok)

    own = attend_own(draft_rows, payload, reach, w_key_up, w_value_up, heads)
    parts = trade_blocks(fold_blocks(partial, count), count)
    mine, other = sum_heads(project_out(w_out, own, parts, heads, tok))
    resid, moe_in = norm(hidden_in, mine, other, moe_gain, packed)

    (radix, stride), *rest = phases(count)
    near, half, mid = rest[-1][1], 1 << (len(rest) - 1), radix // 2
    weights = (w_gate, w_up, w_down)
    first = [swap(moe_in, "blk", stride * j) for j in range(1, radix)]
    mine = [moe_in[None]]
    for _, step in rest[:-1]:
        mine = mine + [swap(t, "blk", step) for t in mine]
    first[-1] = after(first[-1], *mine[1:])
    others = [jnp.stack(first)]
    for _, step in rest[:-1]:
        others = others + [swap(t, "blk", step) for t in others]
    tokens = [list(pair) for pair in zip(mine, others)]
    kept, sent = [], []
    cuts = [mid] + [1] * (radix - mid)
    for i in range(half):
        pair = tokens[i]
        if i:
            pair[1] = after(pair[1], kept[-1][0], sent[-1][0])
        far = [swap(t, "blk", near) for t in pair]
        tokens.append(far)
        places = [at * radix + j for at in (i, i + half) for j in range(radix)]
        inner = cuts if i + 1 == half else [radix]
        done = list(expert(pair + far, places, mix, weights, cuts + inner))
        kept.append(done[: len(cuts)])
        sent.append(done[len(cuts) :])
    order = [*range(1, len(cuts)), 0]
    sums = []
    for i in range(half):
        if i + 1 == half:
            got = [None] * len(cuts)
            for at in order:
                got[at] = swap(sent[i][at], "blk", near)
        else:
            got = swap(sent[i][0], "blk", near)
            got = [got[:mid]] + [got[j : j + 1] for j in range(mid, radix)]
        sums.append([add16(k, g) for k, g in zip(kept[i], got)])
    for _, step in reversed(rest[:-1]):
        part = len(sums) // 2
        for i in range(part):
            lead = swap(sums[part + i][order[0]], "blk", step)
            got = [None] * len(order)
            got[order[0]] = lead
            for at in order[1:]:
                got[at] = swap(after(sums[part + i][at], lead), "blk", step)
            sums[part + i] = got
        got = sums[part:]
        for i in range(part):
            last = None
            for at in order:
                value = got[i][at] if last is None else after(got[i][at], last)
                last = sums[i][at] = add16(sums[i][at], value)
        sums = sums[:part]
    (sums,) = sums
    back = [swap(sums[at][0], "blk", stride * (mid + at - 1)) for at in order[:-1]]
    back += [swap(sums[0][j], "blk", stride * j) for j in range(1, mid)]
    total = sums[0][0].astype(f32)
    for value in reversed(back):
        total = total + value.astype(f32)
    mine, other = sum_heads(total.astype(bf16))
    layer_out = (resid.astype(f32) + (mine.astype(f32) + other.astype(f32))).astype(bf16)
    pieces = [piece for group in tokens for piece in group]
    new_rows = place_rows(index, pieces, accepted.shape[1], hidden_in.shape[1])
    return (layer_out, new_rows)


def solution(mesh):
    return jax.shard_map(
        shards,
        mesh=mesh,
        in_specs=(
            P("blk", None),
            P(),
            P("head", None),
            P("head", None),
            P(),
            P(None, "head"),
            P(None, "head"),
            P("head", None),
            P("blk", None),
            P("blk"),
            P("blk"),
            P(),
            P("blk", None),
            P("blk", None),
            P("blk", None),
            P(),
            P("blk", None),
            P("blk", None),
            P("blk", "head", None),
            P("blk", "head", None),
            P("blk", "head", None),
        ),
        out_specs=(P("blk", None), P("blk", None)),
        check_vma=False,
    )
```

```python
import functools

import jax
import jax.numpy as jnp
from jax import lax
from jax.experimental import pallas as pl
from jax.experimental.pallas import tpu as pltpu
from jax.sharding import PartitionSpec as P

NOPE = 128
ROPE = 64
HALF = ROPE // 2
VDIM = 128
RANK = 512
NEW_DEV = 16
LANES = 128

EPSILON = 1e-06
ROUTE_SCALE = 2.446
ROPE_BASE = 50000.0
MIB = 1 << 20

f32 = jnp.float32
bf16 = jnp.bfloat16


def params(mib):
    return pltpu.CompilerParams(vmem_limit_bytes=mib * MIB)


def cost(flops, nbytes, trans=0):
    return pl.CostEstimate(flops=flops, bytes_accessed=nbytes, transcendentals=trans)


def nt(left, right):
    return lax.dot_general(left, right, (((1,), (1,)), ((), ())), preferred_element_type=f32)


def nn(left, right):
    return jnp.dot(left, right, preferred_element_type=f32)


def phases(count):
    out, stride = [], count
    while stride > 1:
        radix = 4 if stride == count and count >= 4 else 2
        stride //= radix
        out.append((radix, stride))
    return out


def swap(value, axis, bit):
    count = lax.axis_size(axis)
    return lax.ppermute(value, axis, [(i, i ^ bit) for i in range(count)])


def gather_blocks(value, count):
    (radix, stride), *rest = phases(count)
    pieces = [jnp.stack([value] + [swap(value, "blk", stride * j) for j in range(1, radix)])]
    for _, stride in rest:
        pieces = pieces + [swap(p, "blk", stride) for p in pieces]
    return pieces


def after(value, *others):
    return lax.optimization_barrier((value, *others))[0]


def add16(left, right):
    return (left.astype(f32) + right.astype(f32)).astype(bf16)


def fold_blocks(pieces, count):
    for _, stride in reversed(phases(count)[1:]):
        half = len(pieces) // 2
        got = [swap(p, "blk", stride) for p in pieces[half:]]
        pieces = [add16(p, g) for p, g in zip(pieces[:half], got)]
    return pieces[0]


def trade_blocks(value, count):
    radix, stride = phases(count)[0]
    return [value[0]] + [swap(value[j], "blk", stride * j) for j in range(1, radix)]


def place_of(relative, count):
    (radix, stride), *rest = phases(count)
    place = relative // stride
    size = radix
    for _, step in rest:
        place = place + (relative // step) % 2 * size
        size *= 2
    return place


def pre_kernel(
    heads, experts, query_hbm, parents_hbm, lengths_hbm, routes_hbm, logits_hbm, hidden_hbm, gain_hbm,
    out_ref, normed_ref, trig_ref, reach_ref, wq, parents_ref, len_ref, routes_ref,
    logits_ref, hidden_ref, gain_ref, sems,
):
    copies = [
        pltpu.make_async_copy(src, dst, sems.at[i])
        for i, (src, dst) in enumerate((
            (query_hbm, wq), (parents_hbm, parents_ref), (lengths_hbm, len_ref),
            (routes_hbm, routes_ref), (logits_hbm, logits_ref), (hidden_hbm, hidden_ref),
            (gain_hbm, gain_ref),
        ))
    ]
    for copy in copies[1:] + copies[:1]:
        copy.start()
    for copy in copies[1:]:
        copy.wait()
    tok = hidden_ref.shape[0]
    rows = lax.broadcasted_iota(jnp.int32, (tok, tok), 0)
    cols = lax.broadcasted_iota(jnp.int32, (tok, tok), 1)
    eye = (rows == cols).astype(f32)
    below = jnp.where(rows == parents_ref[...], 1.0, 0.0) + eye
    for _ in range(max(1, (tok - 1).bit_length())):
        step = below.astype(bf16)
        below = jnp.minimum(nn(step, step), 1.0)
    reach = nt(eye.astype(bf16), below.astype(bf16))
    reach_ref[...] = reach
    depth = jnp.sum(reach, axis=-1, keepdims=True) - 1.0
    at = lax.broadcasted_iota(jnp.int32, len_ref.shape, 1) == lax.axis_index("blk")
    length = jnp.sum(jnp.where(at, len_ref[...].astype(f32), 0.0), axis=-1, keepdims=True)
    position = length + depth
    lane = lax.broadcasted_iota(jnp.int32, (1, LANES), 1)
    freqs = ROPE_BASE ** (-2.0 * (lane % HALF).astype(f32) / ROPE)
    angles = position * freqs
    cosine, sine = jnp.cos(angles), jnp.sin(angles)
    trig_ref[:, :LANES] = cosine
    trig_ref[:, LANES:] = sine
    sigma = jax.nn.sigmoid(logits_ref[...])
    weight = ROUTE_SCALE * sigma / jnp.sum(sigma, axis=0, keepdims=True)
    named = lax.broadcasted_iota(jnp.int32, (LANES, 1), 0)
    mix = jnp.zeros((LANES, tok), f32)
    for k in range(weight.shape[0]):
        mix = mix + jnp.where(named % experts == routes_ref[k : k + 1], weight[k : k + 1], 0.0)
    high = mix.astype(bf16).astype(f32)
    mix = jnp.where(named < experts, high, jnp.where(named < 2 * experts, mix - high, 0.0))
    mix = nt(eye.astype(bf16), mix.astype(bf16))
    hidden = hidden_ref[...].astype(f32)
    mean_square = jnp.mean(hidden * hidden, axis=-1, keepdims=True)
    normed = (hidden * lax.rsqrt(mean_square + EPSILON) * gain_ref[...]).astype(bf16)
    copies[0].wait()
    size = NOPE + ROPE
    for h in range(heads):
        part = nt(normed, wq[h * size : h * size + NOPE])
        out_ref[:, h * NOPE : (h + 1) * NOPE] = part.astype(bf16)
    pad = [jnp.zeros((LANES - heads * HALF, wq.shape[1]), bf16)] if heads * HALF < LANES else []
    first, second = (
        nt(normed, jnp.concatenate(
            [wq[h * size + NOPE + at : h * size + NOPE + at + HALF] for h in range(heads)] + pad))
        for at in (0, HALF)
    )
    base = heads * NOPE
    out_ref[:, base : base + LANES] = (first * cosine - second * sine).astype(bf16)
    out_ref[:, base + LANES : base + 2 * LANES] = (second * cosine + first * sine).astype(bf16)
    out_ref[:, base + 2 * LANES :] = mix.astype(bf16)
    normed_ref[...] = normed


def prepare(lengths, hidden, gain, parents, routes, logits, w_query, heads, experts):
    tok, width = hidden.shape
    vmem = pl.BlockSpec(memory_space=pltpu.VMEM)
    hbm = pl.BlockSpec(memory_space=pltpu.HBM)
    lanes = heads * NOPE + 3 * LANES
    args = (w_query, parents, lengths[None], routes.T, logits.T, hidden, gain[None])
    return pl.pallas_call(
        functools.partial(pre_kernel, heads, experts),
        out_shape=(
            jax.ShapeDtypeStruct((tok, lanes), bf16),
            jax.ShapeDtypeStruct((tok, width), bf16),
            jax.ShapeDtypeStruct((tok, 2 * LANES), f32),
            jax.ShapeDtypeStruct((tok, tok), f32),
        ),
        in_specs=[hbm] * len(args),
        out_specs=(vmem,) * 4,
        scratch_shapes=[pltpu.VMEM(a.shape, a.dtype) for a in args]
        + [pltpu.SemaphoreType.DMA((len(args),))],
        compiler_params=params(58),
        cost_estimate=cost(2 * tok * width * 1100, 2 * width * 1100),
        name="prepare",
    )(*args)


def spread(heads):
    row = lax.broadcasted_iota(jnp.int32, (ROPE, 2 * LANES), 0)
    col = lax.broadcasted_iota(jnp.int32, (ROPE, 2 * LANES), 1)
    inside = col % LANES < heads * HALF
    return jnp.where((row == col // LANES * HALF + col % HALF) & inside, 1.0, 0.0).astype(bf16)


def keys_values(rows, key_up, value_up, heads):
    low = rows[:, :RANK]
    nope = nn(low, key_up).astype(bf16)
    rope = nn(rows[:, RANK:], spread(heads)).astype(bf16)
    return jnp.concatenate([nope, rope], axis=-1), nn(low, value_up).astype(bf16)


def expand_kernel(heads, rows_ref, key_ref, value_ref, keys_out, values_out):
    keys_out[...], values_out[...] = keys_values(rows_ref[...], key_ref[...], value_ref[...], heads)


def expand(rows, key_up, value_up, heads):
    vmem = pl.BlockSpec(memory_space=pltpu.VMEM)
    count = rows.shape[0]
    return pl.pallas_call(
        functools.partial(expand_kernel, heads),
        out_shape=(
            jax.ShapeDtypeStruct((count, heads * NOPE + 2 * LANES), bf16),
            jax.ShapeDtypeStruct((count, heads * VDIM), bf16),
        ),
        in_specs=[vmem] * 3,
        out_specs=(vmem,) * 2,
        compiler_params=params(16),
        cost_estimate=cost(4 * count * RANK * heads * NOPE, 4 * count * RANK),
        name="expand",
    )(rows, key_up, value_up)


def by_head(query, heads):
    tok, lanes = query.shape[0], heads * NOPE + 2 * LANES
    lane = lax.broadcasted_iota(jnp.int32, (1, lanes), 1)
    head = jnp.where(lane < heads * NOPE, lane // NOPE, lane % LANES // HALF)
    query = query[:, :lanes].astype(f32)
    return jnp.concatenate(
        [jnp.where(head == h, query, 0.0) for h in range(heads)], axis=0
    ).astype(bf16)


def attend(query, keys, values, seen, heads):
    tok = query.shape[0] // heads
    scale = (NOPE + ROPE) ** (-0.5)
    weight = jnp.where(seen, jnp.exp(nt(query, keys) * scale), 0.0)
    high = weight.astype(bf16)
    low = (weight - high.astype(f32)).astype(bf16)
    full = nn(high, values)
    numer = jnp.concatenate(
        [full[h * tok : (h + 1) * tok, h * VDIM : (h + 1) * VDIM] for h in range(heads)], axis=0
    )
    ones = jnp.ones((16, keys.shape[0]), bf16)
    denom = nt(ones, high) + nt(ones, low)
    if denom.shape[1] < LANES:
        denom = jnp.concatenate([denom, jnp.zeros((16, LANES - denom.shape[1]), f32)], axis=-1)
    return jnp.concatenate([numer, denom], axis=0)


def slots_kernel(
    heads, slots, block, pieces, experts, place_ref, live_ref, index_ref, keys_ref, values_ref, *refs
):
    queries, outs, mix = refs[:pieces], refs[pieces : 2 * pieces], refs[2 * pieces]
    each, tok, lanes = queries[0].shape
    named = lax.broadcasted_iota(jnp.int32, (1, LANES), 1)
    mine = (named == index_ref[0]) | (named == index_ref[0] + experts)
    for i, query in enumerate(queries):
        shares = query[:, :, lanes - LANES :].reshape(each * tok, LANES).astype(f32)
        share = jnp.sum(jnp.where(mine, shares, 0.0), axis=-1, keepdims=True)
        mix[i * each : (i + 1) * each] = share.reshape(each, tok, 1)
    for out in outs:
        out[...] = jnp.zeros(out.shape, out.dtype)
    parts = []
    lane = lax.broadcasted_iota(jnp.int32, (1, block), 1)
    for s in range(slots):
        place = place_ref[s]
        query = queries[0][place % each]
        for p in range(1, pieces):
            query = jnp.where(place // each == p, queries[p][place % each], query)
        keys, values = (r[s * block : (s + 1) * block] for r in (keys_ref, values_ref))
        parts.append(attend(by_head(query, heads), keys, values, lane < live_ref[s], heads))
    for s in range(slots):
        place = place_ref[s]
        total = parts[s]
        for other in range(slots):
            if other != s:
                total = total + jnp.where(place_ref[other] == place, parts[other], 0.0)
        for p, out in enumerate(outs):
            @pl.when(place // each == p)
            def _():
                out[place % each] = total.astype(bf16)


def attend_slots(place, live, index, keys, values, queries, heads, block, experts):
    smem = pl.BlockSpec(memory_space=pltpu.SMEM)
    vmem = pl.BlockSpec(memory_space=pltpu.VMEM)
    slots, each, tok = place.shape[0], queries[0].shape[0], queries[0].shape[1]
    pieces = len(queries)
    out = jax.ShapeDtypeStruct((each, heads * tok + 16, LANES), bf16)
    mix = jax.ShapeDtypeStruct((pieces * each, tok, 1), f32)
    results = pl.pallas_call(
        functools.partial(slots_kernel, heads, slots, block, pieces, experts),
        out_shape=(out,) * pieces + (mix,),
        in_specs=[smem, smem, smem, vmem, vmem] + [vmem] * pieces,
        out_specs=(vmem,) * (pieces + 1),
        compiler_params=params(24),
        cost_estimate=cost(1 << 28, 2 << 20),
        name="attend_slots",
    )(place, live, index, keys, values, *queries)
    return list(results[:pieces]), results[pieces]


def own_kernel(heads, rows_ref, query_ref, reach_ref, key_ref, value_ref, out_ref):
    keys, values = keys_values(rows_ref[...], key_ref[...], value_ref[...], heads)
    seen = jnp.concatenate([reach_ref[...]] * heads, axis=0) > 0.5
    out_ref[...] = attend(by_head(query_ref[...], heads), keys, values, seen, heads)


def attend_own(rows, query, reach, key_up, value_up, heads):
    vmem = pl.BlockSpec(memory_space=pltpu.VMEM)
    return pl.pallas_call(
        functools.partial(own_kernel, heads),
        out_shape=jax.ShapeDtypeStruct((heads * rows.shape[0] + 16, LANES), f32),
        in_specs=[vmem] * 5,
        out_specs=vmem,
        compiler_params=params(16),
        cost_estimate=cost(1 << 26, 2 << 20),
        name="attend_own",
    )(rows, query, reach, key_up, value_up)


def project_kernel(heads, parts, w_ref, own_ref, *refs):
    total = own_ref[...]
    for ref in refs[:parts]:
        total = total + ref[...].astype(f32)
    count = heads * (total.shape[0] - 16) // heads
    tok = count // heads
    row = lax.broadcasted_iota(jnp.int32, (count, LANES), 0)
    col = lax.broadcasted_iota(jnp.int32, (count, LANES), 1)
    denom = jnp.sum(jnp.where(row == col, total[count : count + 1], 0.0), axis=-1, keepdims=True)
    attended = (total[:count] / denom).astype(bf16)
    wide = jnp.concatenate([attended[h * tok : (h + 1) * tok] for h in range(heads)], axis=-1)
    refs[parts][...] = nn(wide, w_ref[...]).astype(bf16)


def project_out(w_out, own, parts, heads, tok):
    vmem = pl.BlockSpec(memory_space=pltpu.VMEM)
    return pl.pallas_call(
        functools.partial(project_kernel, heads, len(parts)),
        out_shape=jax.ShapeDtypeStruct((tok, w_out.shape[1]), bf16),
        in_specs=[vmem] * (2 + len(parts)),
        out_specs=vmem,
        compiler_params=params(16),
        cost_estimate=cost(2 * tok * w_out.size, 2 * w_out.size),
        name="project_out",
    )(w_out, own, *parts)


def norm_kernel(hidden_ref, mine_ref, other_ref, gain_ref, packed_ref, resid_ref, out_ref):
    added = mine_ref[...].astype(f32) + other_ref[...].astype(f32)
    resid = (hidden_ref[...].astype(f32) + added).astype(bf16)
    resid_ref[...] = resid
    value = resid.astype(f32)
    mean_square = jnp.mean(value * value, axis=-1, keepdims=True)
    width = value.shape[1]
    out_ref[:, :width] = (value * lax.rsqrt(mean_square + EPSILON) * gain_ref[...]).astype(bf16)
    out_ref[:, width:] = packed_ref[...]


def norm(hidden, mine, other, gain, packed):
    tok, width = hidden.shape
    vmem = pl.BlockSpec(memory_space=pltpu.VMEM)
    return pl.pallas_call(
        norm_kernel,
        out_shape=(
            jax.ShapeDtypeStruct((tok, width), bf16),
            jax.ShapeDtypeStruct((tok, width + packed.shape[1]), bf16),
        ),
        in_specs=[vmem] * 5,
        out_specs=(vmem, vmem),
        compiler_params=params(8),
        name="norm",
    )(hidden, mine, other, gain[None], packed)


def expert_kernel(parts, cuts, *refs):
    blocks = sum(cuts)
    tokens, mixes, outs = refs[:parts], refs[parts : parts + blocks], refs[parts + blocks + 3 :]
    gate, up, down = refs[parts + blocks : parts + blocks + 3]
    tok, width = tokens[0].shape[1:]
    rows = jnp.concatenate([r[i] for r in tokens for i in range(r.shape[0])], axis=0)
    weight = jnp.concatenate([m[0] for m in mixes], axis=0)
    gated = nt(rows, gate[0])
    gated = gated / (1.0 + jnp.exp(-gated))
    act = (gated * nt(rows, up[0])).astype(bf16)
    out = (nn(act, down[0]) * weight).astype(bf16)
    at = 0
    for ref, size in zip(outs, cuts):
        ref[...] = out[at * tok : (at + size) * tok].reshape(size, tok, width)
        at += size


def expert(tokens, places, mix, weights, cuts):
    vmem = pl.BlockSpec(memory_space=pltpu.VMEM)
    parts, size = len(tokens), weights[0].size
    tok, width = tokens[0].shape[1], weights[0].shape[2]
    blocks = [pl.BlockSpec((t.shape[0], tok, width), lambda i: (0, 0, 0)) for t in tokens]
    shares = [pl.BlockSpec((1, tok, 1), lambda i, at=at: (at, 0, 0)) for at in places]
    return pl.pallas_call(
        functools.partial(expert_kernel, parts, cuts),
        grid=(1,),
        out_shape=tuple(jax.ShapeDtypeStruct((cut, tok, width), bf16) for cut in cuts),
        in_specs=blocks + shares + [vmem] * len(weights),
        out_specs=tuple(pl.BlockSpec((cut, tok, width), lambda i: (0, 0, 0)) for cut in cuts),
        compiler_params=params(20),
        cost_estimate=cost(1, 1),
        name="expert",
    )(*tokens, *(mix for _ in places), *weights)


def pack_rows(rows, tok):
    count, width = rows.shape
    lanes = -(-width // (tok // count * LANES)) * LANES
    rows = jnp.pad(rows, ((0, 0), (0, tok // count * lanes - width)))
    return jnp.concatenate([rows[:, at : at + lanes] for at in range(0, rows.shape[1], lanes)])


def rows_kernel(count, index_ref, *refs):
    out_ref = refs[-1]
    target = index_ref[0] * NEW_DEV + lax.broadcasted_iota(jnp.int32, (1, NEW_DEV), 1)
    width = out_ref.shape[1]
    rows = []
    for wide in [ref[i].astype(f32) for ref in refs[:-1] for i in range(ref.shape[0])]:
        parts = [wide[at : at + count] for at in range(0, wide.shape[0], count)]
        rows.append(jnp.concatenate(parts, axis=-1))
    rows = jnp.concatenate(rows, axis=0)
    slot = (rows[:, width : width + 1] * 256.0 + rows[:, width + 1 : width + 2]).astype(jnp.int32)
    here = jnp.where(slot == target, 1.0, 0.0).astype(bf16)
    out_ref[...] = lax.dot_general(
        here, rows[:, :width].astype(bf16), (((0,), (0,)), ((), ())), preferred_element_type=f32
    ).astype(bf16)


def place_rows(index, pieces, count, width):
    smem = pl.BlockSpec(memory_space=pltpu.SMEM)
    out = (NEW_DEV, (RANK + ROPE) // 2)
    lanes = pieces[0].shape[2] - width
    blocks = [pl.BlockSpec((*p.shape[:2], lanes), lambda i: (0, 0, width // lanes)) for p in pieces]
    return pl.pallas_call(
        functools.partial(rows_kernel, count),
        grid=(1,),
        out_shape=jax.ShapeDtypeStruct(out, bf16),
        in_specs=[smem] + blocks,
        out_specs=pl.BlockSpec(out, lambda i: (0, 0)),
        compiler_params=params(8),
        name="place_rows",
    )(index, *pieces)


def sum_heads(value):
    count, bit = lax.axis_size("head"), 1
    other = swap(value, "head", bit)
    while 2 * bit < count:
        bit *= 2
        value = add16(value, other)
        other = swap(value, "head", bit)
    return value, other


def join_heads(value):
    if lax.axis_size("head") == 2:
        other = swap(value, "head", 1)
        first = lax.axis_index("head") == 0
        parts = [jnp.where(first, value, other), jnp.where(first, other, value)]
        return jnp.concatenate(parts, axis=1)
    return lax.all_gather(value, "head", axis=1, tiled=True)


def shards(
    hidden_in, attn_gain, w_query, w_latent, kv_gain, w_key_up, w_value_up, w_out, cache_rows,
    slot_request, slot_block, lengths, parents, accepted, new_slots, moe_gain, routes,
    route_logits, w_gate, w_up, w_down,
):
    count = lax.axis_size("blk")
    me = lax.axis_index("blk").astype(jnp.int32)
    tok = hidden_in.shape[0]
    heads = w_key_up.shape[1] // NOPE
    experts = w_gate.shape[0] * count
    index = me[None]
    payload, normed, trig, reach = prepare(
        lengths, hidden_in, attn_gain, parents, routes, route_logits, w_query,
        heads, experts,
    )
    queries = gather_blocks(payload, count)

    compressed = join_heads(nt(normed, w_latent))
    low = compressed[:, :RANK]
    low = low * lax.rsqrt(jnp.mean(low * low, axis=-1, keepdims=True) + EPSILON) * kv_gain
    first, second = compressed[:, RANK : RANK + HALF], compressed[:, RANK + HALF :]
    cosine, sine = trig[:, :HALF], trig[:, LANES : LANES + HALF]
    draft_rows = jnp.concatenate(
        [low, first * cosine - second * sine, second * cosine + first * sine], axis=-1
    ).astype(bf16)

    keys, values = expand(cache_rows, w_key_up, w_value_up, heads)
    slots = slot_request.shape[0]
    block = cache_rows.shape[0] // slots
    owner = jnp.maximum(slot_request, 0)
    owner_length = jnp.sum(
        jnp.where(owner[:, None] == jnp.arange(lengths.shape[0])[None, :], lengths[None, :], 0), axis=1
    )
    live = jnp.where(slot_request >= 0, owner_length - slot_block * block, 0)
    place = place_of(owner ^ me, count)
    partial, mix = attend_slots(place, live, index, keys, values, queries, heads, block, experts)
    node = jnp.arange(tok, dtype=jnp.int32)
    pick = (accepted.reshape(-1)[:, None] == node[None, :]).astype(bf16)
    chosen = jnp.dot(pick, draft_rows, preferred_element_type=f32).astype(bf16)
    target = new_slots.reshape(-1, 1)
    tail = jnp.concatenate([target // 256, target % 256], axis=1).astype(bf16)
    span = (RANK + ROPE) // 2
    odd = lax.axis_index("head") % 2 == 1
    share = jnp.where(odd, chosen[:, span:], chosen[:, :span])
    packed = pack_rows(jnp.concatenate([share, tail], axis=1), tok)

    own = attend_own(draft_rows, payload, reach, w_key_up, w_value_up, heads)
    parts = trade_blocks(fold_blocks(partial, count), count)
    mine, other = sum_heads(project_out(w_out, own, parts, heads, tok))
    resid, moe_in = norm(hidden_in, mine, other, moe_gain, packed)

    (radix, stride), *rest = phases(count)
    near, half, mid = rest[-1][1], 1 << (len(rest) - 1), radix // 2
    weights = (w_gate, w_up, w_down)
    first = [swap(moe_in, "blk", stride * j) for j in range(1, radix)]
    mine = [moe_in[None]]
    for _, step in rest[:-1]:
        mine = mine + [swap(t, "blk", step) for t in mine]
    first[-1] = after(first[-1], *mine[1:])
    others = [jnp.stack(first)]
    for _, step in rest[:-1]:
        others = others + [swap(t, "blk", step) for t in others]
    tokens = [list(pair) for pair in zip(mine, others)]
    kept, sent = [], []
    cuts = [mid] + [1] * (radix - mid)
    for i in range(half):
        pair = tokens[i]
        if i:
            pair[1] = after(pair[1], kept[-1][0], sent[-1][0])
        far = [swap(t, "blk", near) for t in pair]
        tokens.append(far)
        places = [at * radix + j for at in (i, i + half) for j in range(radix)]
        inner = cuts if i + 1 == half else [radix]
        done = list(expert(pair + far, places, mix, weights, cuts + inner))
        kept.append(done[: len(cuts)])
        sent.append(done[len(cuts) :])
    order = [*range(1, len(cuts)), 0]
    sums = []
    for i in range(half):
        if i + 1 == half:
            got = [None] * len(cuts)
            for at in order:
                got[at] = swap(sent[i][at], "blk", near)
        else:
            got = swap(sent[i][0], "blk", near)
            got = [got[:mid]] + [got[j : j + 1] for j in range(mid, radix)]
        sums.append([add16(k, g) for k, g in zip(kept[i], got)])
    for _, step in reversed(rest[:-1]):
        part = len(sums) // 2
        for i in range(part):
            lead = swap(sums[part + i][order[0]], "blk", step)
            got = [None] * len(order)
            got[order[0]] = lead
            for at in order[1:]:
                got[at] = swap(after(sums[part + i][at], lead), "blk", step)
            sums[part + i] = got
        got = sums[part:]
        for i in range(part):
            last = None
            for at in order:
                value = got[i][at] if last is None else after(got[i][at], last)
                last = sums[i][at] = add16(sums[i][at], value)
        sums = sums[:part]
    (sums,) = sums
    back = [swap(sums[at][0], "blk", stride * (mid + at - 1)) for at in order[:-1]]
    back += [swap(sums[0][j], "blk", stride * j) for j in range(1, mid)]
    total = sums[0][0].astype(f32)
    for value in reversed(back):
        total = total + value.astype(f32)
    mine, other = sum_heads(total.astype(bf16))
    layer_out = (resid.astype(f32) + (mine.astype(f32) + other.astype(f32))).astype(bf16)
    pieces = [piece for group in tokens for piece in group]
    share = place_rows(index, pieces, accepted.shape[1], hidden_in.shape[1])
    other = swap(share, "head", 1)
    new_rows = jnp.concatenate([jnp.where(odd, other, share), jnp.where(odd, share, other)], axis=1)
    return (layer_out, new_rows)


def solution(mesh):
    return jax.shard_map(
        shards,
        mesh=mesh,
        in_specs=(
            P("blk", None),
            P(),
            P("head", None),
            P("head", None),
            P(),
            P(None, "head"),
            P(None, "head"),
            P("head", None),
            P("blk", None),
            P("blk"),
            P("blk"),
            P(),
            P("blk", None),
            P("blk", None),
            P("blk", None),
            P(),
            P("blk", None),
            P("blk", None),
            P("blk", "head", None),
            P("blk", "head", None),
            P("blk", "head", None),
        ),
        out_specs=(P("blk", None), P("blk", None)),
        check_vma=False,
    )
```

```python
import functools

import jax
import jax.numpy as jnp
from jax import lax
from jax.experimental import pallas as pl
from jax.experimental.pallas import tpu as pltpu
from jax.sharding import PartitionSpec as P

NOPE = 128
ROPE = 64
HALF = ROPE // 2
VDIM = 128
RANK = 512
NEW_DEV = 16
LANES = 128

EPSILON = 1e-06
ROUTE_SCALE = 2.446
ROPE_BASE = 50000.0
MIB = 1 << 20

f32 = jnp.float32
bf16 = jnp.bfloat16


def params(mib):
    return pltpu.CompilerParams(vmem_limit_bytes=mib * MIB)


def cost(flops, nbytes, trans=0):
    return pl.CostEstimate(flops=flops, bytes_accessed=nbytes, transcendentals=trans)


def nt(left, right):
    return lax.dot_general(left, right, (((1,), (1,)), ((), ())), preferred_element_type=f32)


def nn(left, right):
    return jnp.dot(left, right, preferred_element_type=f32)


def phases(count):
    out, stride = [], count
    while stride > 1:
        radix = 4 if stride == count and count >= 4 else 2
        stride //= radix
        out.append((radix, stride))
    return out


def swap(value, axis, bit):
    count = lax.axis_size(axis)
    return lax.ppermute(value, axis, [(i, i ^ bit) for i in range(count)])


def gather_blocks(value, count):
    (radix, stride), *rest = phases(count)
    pieces = [jnp.stack([value] + [swap(value, "blk", stride * j) for j in range(1, radix)])]
    for _, stride in rest:
        pieces = pieces + [swap(p, "blk", stride) for p in pieces]
    return pieces


def after(value, *others):
    return lax.optimization_barrier((value, *others))[0]


def add16(left, right):
    return (left.astype(f32) + right.astype(f32)).astype(bf16)


def fold_blocks(pieces, count):
    for _, stride in reversed(phases(count)[1:]):
        half = len(pieces) // 2
        got = [swap(p, "blk", stride) for p in pieces[half:]]
        pieces = [add16(p, g) for p, g in zip(pieces[:half], got)]
    return pieces[0]


def trade_blocks(value, count):
    radix, stride = phases(count)[0]
    return [value[0]] + [swap(value[j], "blk", stride * j) for j in range(1, radix)]


def place_of(relative, count):
    (radix, stride), *rest = phases(count)
    place = relative // stride
    size = radix
    for _, step in rest:
        place = place + (relative // step) % 2 * size
        size *= 2
    return place


def pre_kernel(
    heads, experts, query_hbm, parents_hbm, lengths_hbm, routes_hbm, logits_hbm, hidden_hbm, gain_hbm,
    out_ref, normed_ref, trig_ref, reach_ref, wq, parents_ref, len_ref, routes_ref,
    logits_ref, hidden_ref, gain_ref, sems,
):
    copies = [
        pltpu.make_async_copy(src, dst, sems.at[i])
        for i, (src, dst) in enumerate((
            (query_hbm, wq), (parents_hbm, parents_ref), (lengths_hbm, len_ref),
            (routes_hbm, routes_ref), (logits_hbm, logits_ref), (hidden_hbm, hidden_ref),
            (gain_hbm, gain_ref),
        ))
    ]
    for copy in copies[1:] + copies[:1]:
        copy.start()
    for copy in copies[1:]:
        copy.wait()
    tok = hidden_ref.shape[0]
    rows = lax.broadcasted_iota(jnp.int32, (tok, tok), 0)
    cols = lax.broadcasted_iota(jnp.int32, (tok, tok), 1)
    eye = (rows == cols).astype(f32)
    below = jnp.where(rows == parents_ref[...], 1.0, 0.0) + eye
    for _ in range(max(1, (tok - 1).bit_length())):
        step = below.astype(bf16)
        below = jnp.minimum(nn(step, step), 1.0)
    reach = nt(eye.astype(bf16), below.astype(bf16))
    reach_ref[...] = reach
    depth = jnp.sum(reach, axis=-1, keepdims=True) - 1.0
    at = lax.broadcasted_iota(jnp.int32, len_ref.shape, 1) == lax.axis_index("blk")
    length = jnp.sum(jnp.where(at, len_ref[...].astype(f32), 0.0), axis=-1, keepdims=True)
    position = length + depth
    lane = lax.broadcasted_iota(jnp.int32, (1, LANES), 1)
    freqs = ROPE_BASE ** (-2.0 * (lane % HALF).astype(f32) / ROPE)
    angles = position * freqs
    cosine, sine = jnp.cos(angles), jnp.sin(angles)
    trig_ref[:, :LANES] = cosine
    trig_ref[:, LANES:] = sine
    sigma = jax.nn.sigmoid(logits_ref[...])
    weight = ROUTE_SCALE * sigma / jnp.sum(sigma, axis=0, keepdims=True)
    named = lax.broadcasted_iota(jnp.int32, (LANES, 1), 0)
    mix = jnp.zeros((LANES, tok), f32)
    for k in range(weight.shape[0]):
        mix = mix + jnp.where(named % experts == routes_ref[k : k + 1], weight[k : k + 1], 0.0)
    high = mix.astype(bf16).astype(f32)
    mix = jnp.where(named < experts, high, jnp.where(named < 2 * experts, mix - high, 0.0))
    mix = nt(eye.astype(bf16), mix.astype(bf16))
    hidden = hidden_ref[...].astype(f32)
    mean_square = jnp.mean(hidden * hidden, axis=-1, keepdims=True)
    normed = (hidden * lax.rsqrt(mean_square + EPSILON) * gain_ref[...]).astype(bf16)
    copies[0].wait()
    size = NOPE + ROPE
    for h in range(heads):
        part = nt(normed, wq[h * size : h * size + NOPE])
        out_ref[:, h * NOPE : (h + 1) * NOPE] = part.astype(bf16)
    pad = [jnp.zeros((LANES - heads * HALF, wq.shape[1]), bf16)] if heads * HALF < LANES else []
    first, second = (
        nt(normed, jnp.concatenate(
            [wq[h * size + NOPE + at : h * size + NOPE + at + HALF] for h in range(heads)] + pad))
        for at in (0, HALF)
    )
    base = heads * NOPE
    out_ref[:, base : base + LANES] = (first * cosine - second * sine).astype(bf16)
    out_ref[:, base + LANES : base + 2 * LANES] = (second * cosine + first * sine).astype(bf16)
    out_ref[:, base + 2 * LANES :] = mix.astype(bf16)
    normed_ref[...] = normed


def prepare(lengths, hidden, gain, parents, routes, logits, w_query, heads, experts):
    tok, width = hidden.shape
    vmem = pl.BlockSpec(memory_space=pltpu.VMEM)
    hbm = pl.BlockSpec(memory_space=pltpu.HBM)
    lanes = heads * NOPE + 3 * LANES
    args = (w_query, parents, lengths[None], routes.T, logits.T, hidden, gain[None])
    return pl.pallas_call(
        functools.partial(pre_kernel, heads, experts),
        out_shape=(
            jax.ShapeDtypeStruct((tok, lanes), bf16),
            jax.ShapeDtypeStruct((tok, width), bf16),
            jax.ShapeDtypeStruct((tok, 2 * LANES), f32),
            jax.ShapeDtypeStruct((tok, tok), f32),
        ),
        in_specs=[hbm] * len(args),
        out_specs=(vmem,) * 4,
        scratch_shapes=[pltpu.VMEM(a.shape, a.dtype) for a in args]
        + [pltpu.SemaphoreType.DMA((len(args),))],
        compiler_params=params(58),
        cost_estimate=cost(2 * tok * width * 1100, 2 * width * 1100),
        name="prepare",
    )(*args)


def spread(heads):
    row = lax.broadcasted_iota(jnp.int32, (ROPE, 2 * LANES), 0)
    col = lax.broadcasted_iota(jnp.int32, (ROPE, 2 * LANES), 1)
    inside = col % LANES < heads * HALF
    return jnp.where((row == col // LANES * HALF + col % HALF) & inside, 1.0, 0.0).astype(bf16)


def keys_values(rows, key_up, value_up, heads):
    low = rows[:, :RANK]
    nope = nn(low, key_up).astype(bf16)
    rope = nn(rows[:, RANK:], spread(heads)).astype(bf16)
    return jnp.concatenate([nope, rope], axis=-1), nn(low, value_up).astype(bf16)


def expand_kernel(heads, rows_ref, key_ref, value_ref, keys_out, values_out):
    keys_out[...], values_out[...] = keys_values(rows_ref[...], key_ref[...], value_ref[...], heads)


def expand(rows, key_up, value_up, heads):
    vmem = pl.BlockSpec(memory_space=pltpu.VMEM)
    count = rows.shape[0]
    return pl.pallas_call(
        functools.partial(expand_kernel, heads),
        out_shape=(
            jax.ShapeDtypeStruct((count, heads * NOPE + 2 * LANES), bf16),
            jax.ShapeDtypeStruct((count, heads * VDIM), bf16),
        ),
        in_specs=[vmem] * 3,
        out_specs=(vmem,) * 2,
        compiler_params=params(16),
        cost_estimate=cost(4 * count * RANK * heads * NOPE, 4 * count * RANK),
        name="expand",
    )(rows, key_up, value_up)


def by_head(query, heads):
    tok, lanes = query.shape[0], heads * NOPE + 2 * LANES
    lane = lax.broadcasted_iota(jnp.int32, (1, lanes), 1)
    head = jnp.where(lane < heads * NOPE, lane // NOPE, lane % LANES // HALF)
    query = query[:, :lanes].astype(f32)
    return jnp.concatenate(
        [jnp.where(head == h, query, 0.0) for h in range(heads)], axis=0
    ).astype(bf16)


def attend(query, keys, values, seen, heads):
    tok = query.shape[0] // heads
    scale = (NOPE + ROPE) ** (-0.5)
    weight = jnp.where(seen, jnp.exp(nt(query, keys) * scale), 0.0)
    high = weight.astype(bf16)
    low = (weight - high.astype(f32)).astype(bf16)
    full = nn(high, values)
    numer = jnp.concatenate(
        [full[h * tok : (h + 1) * tok, h * VDIM : (h + 1) * VDIM] for h in range(heads)], axis=0
    )
    ones = jnp.ones((16, keys.shape[0]), bf16)
    denom = nt(ones, high) + nt(ones, low)
    if denom.shape[1] < LANES:
        denom = jnp.concatenate([denom, jnp.zeros((16, LANES - denom.shape[1]), f32)], axis=-1)
    return jnp.concatenate([numer, denom], axis=0)


def slots_kernel(
    heads, slots, block, pieces, experts, place_ref, live_ref, index_ref, keys_ref, values_ref, *refs
):
    queries, outs, mix = refs[:pieces], refs[pieces : 2 * pieces], refs[2 * pieces]
    each, tok, lanes = queries[0].shape
    named = lax.broadcasted_iota(jnp.int32, (1, LANES), 1)
    mine = (named == index_ref[0]) | (named == index_ref[0] + experts)
    for i, query in enumerate(queries):
        shares = query[:, :, lanes - LANES :].reshape(each * tok, LANES).astype(f32)
        share = jnp.sum(jnp.where(mine, shares, 0.0), axis=-1, keepdims=True)
        mix[i * each : (i + 1) * each] = share.reshape(each, tok, 1)
    for out in outs:
        out[...] = jnp.zeros(out.shape, out.dtype)
    parts = []
    lane = lax.broadcasted_iota(jnp.int32, (1, block), 1)
    for s in range(slots):
        place = place_ref[s]
        query = queries[0][place % each]
        for p in range(1, pieces):
            query = jnp.where(place // each == p, queries[p][place % each], query)
        keys, values = (r[s * block : (s + 1) * block] for r in (keys_ref, values_ref))
        parts.append(attend(by_head(query, heads), keys, values, lane < live_ref[s], heads))
    for s in range(slots):
        place = place_ref[s]
        total = parts[s]
        for other in range(slots):
            if other != s:
                total = total + jnp.where(place_ref[other] == place, parts[other], 0.0)
        for p, out in enumerate(outs):
            @pl.when(place // each == p)
            def _():
                out[place % each] = total.astype(bf16)


def attend_slots(place, live, index, keys, values, queries, heads, block, experts):
    smem = pl.BlockSpec(memory_space=pltpu.SMEM)
    vmem = pl.BlockSpec(memory_space=pltpu.VMEM)
    slots, each, tok = place.shape[0], queries[0].shape[0], queries[0].shape[1]
    pieces = len(queries)
    out = jax.ShapeDtypeStruct((each, heads * tok + 16, LANES), bf16)
    mix = jax.ShapeDtypeStruct((pieces * each, tok, 1), f32)
    results = pl.pallas_call(
        functools.partial(slots_kernel, heads, slots, block, pieces, experts),
        out_shape=(out,) * pieces + (mix,),
        in_specs=[smem, smem, smem, vmem, vmem] + [vmem] * pieces,
        out_specs=(vmem,) * (pieces + 1),
        compiler_params=params(24),
        cost_estimate=cost(1 << 28, 2 << 20),
        name="attend_slots",
    )(place, live, index, keys, values, *queries)
    return list(results[:pieces]), results[pieces]


def own_kernel(heads, rows_ref, query_ref, reach_ref, key_ref, value_ref, out_ref):
    keys, values = keys_values(rows_ref[...], key_ref[...], value_ref[...], heads)
    seen = jnp.concatenate([reach_ref[...]] * heads, axis=0) > 0.5
    out_ref[...] = attend(by_head(query_ref[...], heads), keys, values, seen, heads)


def attend_own(rows, query, reach, key_up, value_up, heads):
    vmem = pl.BlockSpec(memory_space=pltpu.VMEM)
    return pl.pallas_call(
        functools.partial(own_kernel, heads),
        out_shape=jax.ShapeDtypeStruct((heads * rows.shape[0] + 16, LANES), f32),
        in_specs=[vmem] * 5,
        out_specs=vmem,
        compiler_params=params(16),
        cost_estimate=cost(1 << 26, 2 << 20),
        name="attend_own",
    )(rows, query, reach, key_up, value_up)


def project_kernel(heads, parts, w_ref, own_ref, *refs):
    total = own_ref[...]
    for ref in refs[:parts]:
        total = total + ref[...].astype(f32)
    count = heads * (total.shape[0] - 16) // heads
    tok = count // heads
    row = lax.broadcasted_iota(jnp.int32, (count, LANES), 0)
    col = lax.broadcasted_iota(jnp.int32, (count, LANES), 1)
    denom = jnp.sum(jnp.where(row == col, total[count : count + 1], 0.0), axis=-1, keepdims=True)
    attended = (total[:count] / denom).astype(bf16)
    wide = jnp.concatenate([attended[h * tok : (h + 1) * tok] for h in range(heads)], axis=-1)
    refs[parts][...] = nn(wide, w_ref[...]).astype(bf16)


def project_out(w_out, own, parts, heads, tok):
    vmem = pl.BlockSpec(memory_space=pltpu.VMEM)
    return pl.pallas_call(
        functools.partial(project_kernel, heads, len(parts)),
        out_shape=jax.ShapeDtypeStruct((tok, w_out.shape[1]), bf16),
        in_specs=[vmem] * (2 + len(parts)),
        out_specs=vmem,
        compiler_params=params(16),
        cost_estimate=cost(2 * tok * w_out.size, 2 * w_out.size),
        name="project_out",
    )(w_out, own, *parts)


def norm_kernel(hidden_ref, mine_ref, other_ref, gain_ref, packed_ref, resid_ref, out_ref):
    added = mine_ref[...].astype(f32) + other_ref[...].astype(f32)
    resid = (hidden_ref[...].astype(f32) + added).astype(bf16)
    resid_ref[...] = resid
    value = resid.astype(f32)
    mean_square = jnp.mean(value * value, axis=-1, keepdims=True)
    width = value.shape[1]
    out_ref[:, :width] = (value * lax.rsqrt(mean_square + EPSILON) * gain_ref[...]).astype(bf16)
    out_ref[:, width:] = packed_ref[...]


def norm(hidden, mine, other, gain, packed):
    tok, width = hidden.shape
    vmem = pl.BlockSpec(memory_space=pltpu.VMEM)
    return pl.pallas_call(
        norm_kernel,
        out_shape=(
            jax.ShapeDtypeStruct((tok, width), bf16),
            jax.ShapeDtypeStruct((tok, width + packed.shape[1]), bf16),
        ),
        in_specs=[vmem] * 5,
        out_specs=(vmem, vmem),
        compiler_params=params(8),
        name="norm",
    )(hidden, mine, other, gain[None], packed)


def expert_kernel(parts, cuts, *refs):
    blocks = sum(cuts)
    tokens, mixes, outs = refs[:parts], refs[parts : parts + blocks], refs[parts + blocks + 3 :]
    gate, up, down = refs[parts + blocks : parts + blocks + 3]
    tok, width = tokens[0].shape[1:]
    rows = jnp.concatenate([r[i] for r in tokens for i in range(r.shape[0])], axis=0)
    weight = jnp.concatenate([m[0] for m in mixes], axis=0)
    gated = nt(rows, gate[0])
    gated = gated / (1.0 + jnp.exp(-gated))
    act = (gated * nt(rows, up[0])).astype(bf16)
    out = (nn(act, down[0]) * weight).astype(bf16)
    at = 0
    for ref, size in zip(outs, cuts):
        ref[...] = out[at * tok : (at + size) * tok].reshape(size, tok, width)
        at += size


def expert(tokens, places, mix, weights, cuts):
    vmem = pl.BlockSpec(memory_space=pltpu.VMEM)
    parts, size = len(tokens), weights[0].size
    tok, width = tokens[0].shape[1], weights[0].shape[2]
    blocks = [pl.BlockSpec((t.shape[0], tok, width), lambda i: (0, 0, 0)) for t in tokens]
    shares = [pl.BlockSpec((1, tok, 1), lambda i, at=at: (at, 0, 0)) for at in places]
    return pl.pallas_call(
        functools.partial(expert_kernel, parts, cuts),
        grid=(1,),
        out_shape=tuple(jax.ShapeDtypeStruct((cut, tok, width), bf16) for cut in cuts),
        in_specs=blocks + shares + [vmem] * len(weights),
        out_specs=tuple(pl.BlockSpec((cut, tok, width), lambda i: (0, 0, 0)) for cut in cuts),
        compiler_params=params(20),
        cost_estimate=cost(1, 1),
        name="expert",
    )(*tokens, *(mix for _ in places), *weights)


def pack_rows(rows, tok):
    count, width = rows.shape
    lanes = -(-width // (tok // count * LANES)) * LANES
    rows = jnp.pad(rows, ((0, 0), (0, tok // count * lanes - width)))
    return jnp.concatenate([rows[:, at : at + lanes] for at in range(0, rows.shape[1], lanes)])


def rows_kernel(count, index_ref, *refs):
    out_ref = refs[-1]
    target = index_ref[0] * NEW_DEV + lax.broadcasted_iota(jnp.int32, (1, NEW_DEV), 1)
    width = out_ref.shape[1]
    rows = []
    for wide in [ref[i].astype(f32) for ref in refs[:-1] for i in range(ref.shape[0])]:
        parts = [wide[at : at + count] for at in range(0, wide.shape[0], count)]
        rows.append(jnp.concatenate(parts, axis=-1))
    rows = jnp.concatenate(rows, axis=0)
    slot = (rows[:, width : width + 1] * 256.0 + rows[:, width + 1 : width + 2]).astype(jnp.int32)
    here = jnp.where(slot == target, 1.0, 0.0).astype(bf16)
    out_ref[...] = lax.dot_general(
        here, rows[:, :width].astype(bf16), (((0,), (0,)), ((), ())), preferred_element_type=f32
    ).astype(bf16)


def place_rows(index, pieces, count, width):
    smem = pl.BlockSpec(memory_space=pltpu.SMEM)
    out = (NEW_DEV, (RANK + ROPE) // 2)
    lanes = pieces[0].shape[2] - width
    blocks = [pl.BlockSpec((*p.shape[:2], lanes), lambda i: (0, 0, width // lanes)) for p in pieces]
    return pl.pallas_call(
        functools.partial(rows_kernel, count),
        grid=(1,),
        out_shape=jax.ShapeDtypeStruct(out, bf16),
        in_specs=[smem] + blocks,
        out_specs=pl.BlockSpec(out, lambda i: (0, 0)),
        compiler_params=params(8),
        name="place_rows",
    )(index, *pieces)


def sum_heads(value):
    count, bit = lax.axis_size("head"), 1
    other = swap(value, "head", bit)
    while 2 * bit < count:
        bit *= 2
        value = add16(value, other)
        other = swap(value, "head", bit)
    return value, other


def join_heads(value):
    if lax.axis_size("head") == 2:
        other = swap(value, "head", 1)
        first = lax.axis_index("head") == 0
        parts = [jnp.where(first, value, other), jnp.where(first, other, value)]
        return jnp.concatenate(parts, axis=1)
    return lax.all_gather(value, "head", axis=1, tiled=True)


def shards(
    hidden_in, attn_gain, w_query, w_latent, kv_gain, w_key_up, w_value_up, w_out, cache_rows,
    slot_request, slot_block, lengths, parents, accepted, new_slots, moe_gain, routes,
    route_logits, w_gate, w_up, w_down,
):
    count = lax.axis_size("blk")
    me = lax.axis_index("blk").astype(jnp.int32)
    tok = hidden_in.shape[0]
    heads = w_key_up.shape[1] // NOPE
    experts = w_gate.shape[0] * count
    index = me[None]
    payload, normed, trig, reach = prepare(
        lengths, hidden_in, attn_gain, parents, routes, route_logits, w_query,
        heads, experts,
    )
    queries = gather_blocks(payload, count)

    compressed = join_heads(nt(normed, w_latent))
    low = compressed[:, :RANK]
    low = low * lax.rsqrt(jnp.mean(low * low, axis=-1, keepdims=True) + EPSILON) * kv_gain
    first, second = compressed[:, RANK : RANK + HALF], compressed[:, RANK + HALF :]
    cosine, sine = trig[:, :HALF], trig[:, LANES : LANES + HALF]
    draft_rows = jnp.concatenate(
        [low, first * cosine - second * sine, second * cosine + first * sine], axis=-1
    ).astype(bf16)

    keys, values = expand(cache_rows, w_key_up, w_value_up, heads)
    slots = slot_request.shape[0]
    block = cache_rows.shape[0] // slots
    owner = jnp.maximum(slot_request, 0)
    owner_length = jnp.sum(
        jnp.where(owner[:, None] == jnp.arange(lengths.shape[0])[None, :], lengths[None, :], 0), axis=1
    )
    live = jnp.where(slot_request >= 0, owner_length - slot_block * block, 0)
    place = place_of(owner ^ me, count)
    partial, mix = attend_slots(place, live, index, keys, values, queries, heads, block, experts)
    node = jnp.arange(tok, dtype=jnp.int32)
    pick = (accepted.reshape(-1)[:, None] == node[None, :]).astype(bf16)
    chosen = jnp.dot(pick, draft_rows, preferred_element_type=f32).astype(bf16)
    target = new_slots.reshape(-1, 1)
    tail = jnp.concatenate([target // 256, target % 256], axis=1).astype(bf16)
    span = (RANK + ROPE) // 2
    odd = lax.axis_index("head") % 2 == 1
    share = jnp.where(odd, chosen[:, span:], chosen[:, :span])
    packed = pack_rows(jnp.concatenate([share, tail], axis=1), tok)

    own = attend_own(draft_rows, payload, reach, w_key_up, w_value_up, heads)
    parts = trade_blocks(fold_blocks(partial, count), count)
    mine, other = sum_heads(project_out(w_out, own, parts, heads, tok))
    resid, moe_in = norm(hidden_in, mine, other, moe_gain, packed)

    (radix, stride), *rest = phases(count)
    near, half, mid = rest[-1][1], 1 << (len(rest) - 1), radix // 2
    weights = (w_gate, w_up, w_down)
    first = [swap(moe_in, "blk", stride * j) for j in range(1, radix)]
    mine = [moe_in[None]]
    for _, step in rest[:-1]:
        mine = mine + [swap(t, "blk", step) for t in mine]
    first[-1] = after(first[-1], *mine[1:])
    others = [jnp.stack(first)]
    for _, step in rest[:-1]:
        others = others + [swap(t, "blk", step) for t in others]
    tokens = [list(pair) for pair in zip(mine, others)]
    kept, sent = [], []
    cuts = [mid] + [1] * (radix - mid)
    for i in range(half):
        pair = tokens[i]
        if i:
            pair[1] = after(pair[1], kept[-1][0], sent[-1][0])
        far = [swap(t, "blk", near) for t in pair]
        tokens.append(far)
        places = [at * radix + j for at in (i, i + half) for j in range(radix)]
        inner = cuts if i + 1 == half else [radix]
        done = list(expert(pair + far, places, mix, weights, cuts + inner))
        kept.append(done[: len(cuts)])
        sent.append(done[len(cuts) :])
    order = [*range(1, len(cuts)), 0]
    sums = []
    for i in range(half):
        if i + 1 == half:
            got = [None] * len(cuts)
            for at in order:
                got[at] = swap(sent[i][at], "blk", near)
        else:
            got = swap(sent[i][0], "blk", near)
            got = [got[:mid]] + [got[j : j + 1] for j in range(mid, radix)]
        sums.append([add16(k, g) for k, g in zip(kept[i], got)])
    pieces = [piece for group in tokens for piece in group]
    share = place_rows(index, pieces, accepted.shape[1], hidden_in.shape[1])
    other = swap(share, "head", 1)
    for _, step in reversed(rest[:-1]):
        part = len(sums) // 2
        for i in range(part):
            lead = swap(sums[part + i][order[0]], "blk", step)
            got = [None] * len(order)
            got[order[0]] = lead
            for at in order[1:]:
                got[at] = swap(after(sums[part + i][at], lead), "blk", step)
            sums[part + i] = got
        got = sums[part:]
        for i in range(part):
            last = None
            for at in order:
                value = got[i][at] if last is None else after(got[i][at], last)
                last = sums[i][at] = add16(sums[i][at], value)
        sums = sums[:part]
    (sums,) = sums
    back = [swap(sums[at][0], "blk", stride * (mid + at - 1)) for at in order[:-1]]
    back += [swap(sums[0][j], "blk", stride * j) for j in range(1, mid)]
    total = sums[0][0].astype(f32)
    for value in reversed(back):
        total = total + value.astype(f32)
    total, other = lax.optimization_barrier((total, other))
    new_rows = jnp.concatenate([jnp.where(odd, other, share), jnp.where(odd, share, other)], axis=1)
    mine, other = sum_heads(total.astype(bf16))
    layer_out = (resid.astype(f32) + (mine.astype(f32) + other.astype(f32))).astype(bf16)
    return (layer_out, new_rows)


def solution(mesh):
    return jax.shard_map(
        shards,
        mesh=mesh,
        in_specs=(
            P("blk", None),
            P(),
            P("head", None),
            P("head", None),
            P(),
            P(None, "head"),
            P(None, "head"),
            P("head", None),
            P("blk", None),
            P("blk"),
            P("blk"),
            P(),
            P("blk", None),
            P("blk", None),
            P("blk", None),
            P(),
            P("blk", None),
            P("blk", None),
            P("blk", "head", None),
            P("blk", "head", None),
            P("blk", "head", None),
        ),
        out_specs=(P("blk", None), P("blk", None)),
        check_vma=False,
    )
```
